128 devices in a mesh: pix: 32 (over z, x, core), beam: 4 (over y).
Axes of the slice: x: 4, y: 4, z: 4, core: 2. Of those that a mesh axis runs over, the one named last changes fastest.
Arguments:
- sketch: bfloat16 [512, 128, 256], P('beam', 'pix'), may hold values from -6 to 6
- gains: bfloat16 [2048, 32, 128, 128], P('pix', 'beam'), may hold values from -0.09375 to 0.09375
- coverage: int32 [2048, 32], P('pix', 'beam'), may hold values from 0 to 127
Outputs:
- basis: float32 [512, 128, 256], P('beam', 'pix')
- factor: float32 [256, 256], replicated
The draws below stay inside these ranges and needn't reach their ends.
Inputs may be any that keep to these rules, and one draw needn't show every extreme that they name: `coverage`: entries name beam blocks within the slot's group of 128 blocks; a block may be named by several slots.
All inputs are finite; a program needn't handle non-finite values.
Results may differ from the reference program's by a relative error of at most 0.0011.
Values may be sent and summed in bfloat16 or wider, within the bound.
A program may use at most 192 MiB of HBM per device.

```python
import math
import jax
import jax.numpy as jnp
import numpy as np
from jax import lax

BLOCK = 128
BEAMS = 65536
K = 256
SLOTS_G = 8
BLK = 512
BLK_DEV = 128
TILES = 2048
SLOTS = 32


def touch_ends(array, own_key, smallest, top_value):
    longest = array.shape.index(max(array.shape))
    spots = []
    for shift in (0, 1):
        where = [jax.random.randint(jax.random.fold_in(own_key, axis), (), 0, length) for axis, length in enumerate(array.shape)]
        where[longest] = (where[longest] + shift) % array.shape[longest]
        spots.append(tuple(where))
    return array.at[spots[0]].set(smallest).at[spots[1]].set(top_value)


def block_scale(stream_key, shape, cuts, least, top_value):
    level, own = 1.0, jax.random.fold_in(stream_key, 6)
    for dim, parts in cuts:
        draws = jnp.exp(jax.random.uniform(jax.random.fold_in(own, dim), (parts,), jnp.float32, least / len(cuts), top_value / len(cuts)))
        level = level * jnp.repeat(draws, shape[dim] // parts).reshape([-1 if axis == dim else 1 for axis in range(len(shape))])
    return level


def rank_bounds(amount, slope):
    weights = [(1 << 20) // math.isqrt(rank ** slope) + 1 for rank in range(1, amount + 1)]
    width = 1 + sum(weights) // (1 << 30)
    return np.cumsum(np.array([max(1, weight // width) for weight in weights]))


def ranked(key, shape, number_of, lean):
    listing = rank_bounds(number_of, lean)
    pick = jax.random.randint(jax.random.fold_in(key, 1), shape, 0, int(listing[number_of - 1]))
    standing = jnp.searchsorted(jnp.asarray(listing, jnp.int32), pick, side="right")
    return jax.random.permutation(jax.random.fold_in(key, 2), number_of)[standing].astype(jnp.int32)


def bell_draw(key, extent, deviation, bound, cuts=(), held_as=jnp.bfloat16):
    loudness = block_scale(key, extent, cuts, -0.22, 0.18) if cuts else 1.0
    drawn = jax.random.normal(key, extent, jnp.float32) * deviation * loudness
    return jnp.minimum(jnp.maximum(drawn, -bound), bound).astype(held_as)


def setup_inputs(seed: int = 0) -> dict:
    splits = jax.random.split(jax.random.key(seed), 4)
    sketch = bell_draw(splits[0], (BLK, BLOCK, K), 1.0, 6.0, ((0, 4), (1, 32)))
    gains = bell_draw(splits[1], (TILES, SLOTS, BLOCK, BLOCK), (SLOTS * BLOCK) ** -0.5, 0.09375, ((0, 32), (1, 4)))
    coverage = touch_ends(ranked(splits[2], (TILES, SLOTS), BLK_DEV, 1), jax.random.fold_in(splits[2], 3), 0, BLK_DEV - 1).astype(jnp.int32)
    return {"sketch": sketch, "gains": gains, "coverage": coverage}


def reference(sketch, gains, coverage):
    group_base = jnp.arange(SLOTS, dtype=jnp.int32) // SLOTS_G * BLK_DEV
    global_ids = (coverage + group_base[None, :]).astype(jnp.int32)

    def pixel_pass(args):
        tile_gains, tile_ids = args
        picked = sketch[tile_ids].astype(jnp.float32)
        return jnp.einsum('sab,sbk->ak', tile_gains.astype(jnp.float32), picked)
    pixel_sketch = lax.map(pixel_pass, (gains, global_ids))
    rounded = pixel_sketch.astype(jnp.bfloat16)

    def beam_pass(total, args):
        tile_gains, tile_ids, tile_rows = args
        contrib = jnp.einsum('sab,ak->sbk', tile_gains.astype(jnp.float32), tile_rows.astype(jnp.float32))
        return (total.at[tile_ids].add(contrib), None)
    start = jnp.zeros((BLK, BLOCK, K), jnp.float32)
    range_rows, _ = lax.scan(beam_pass, start, (gains, global_ids, rounded))
    flat = range_rows.reshape(BEAMS, K)
    gram = jnp.dot(flat.T.astype(jnp.float32), flat.astype(jnp.float32), precision=lax.Precision.HIGHEST, preferred_element_type=jnp.float32)
    lower = jnp.linalg.cholesky(gram)
    solved = jax.scipy.linalg.solve_triangular(lower, flat.T, lower=True).T
    scale = jnp.sqrt(jnp.float32(BEAMS))
    return ((solved * scale).reshape(BLK, BLOCK, K), lower.T / scale)
```

```python
import functools

import jax
import jax.numpy as jnp
from jax import lax
from jax.experimental import pallas as pl
from jax.experimental.pallas import tpu as pltpu
from jax.sharding import PartitionSpec as P

BEAMS = 65536
BF = jnp.bfloat16
F32 = jnp.float32
MESH = pl.DeviceIdType.MESH
MIB = 1 << 20


def place():
    pix = lax.axis_index("pix")
    y = lax.axis_index("beam")
    core = lax.rem(pix, 2)
    x = lax.rem(lax.div(pix, 2), 4)
    z = lax.div(pix, 8)
    return pix, y, z, x, core


def step4(v, d):
    return lax.rem(v + d, 4)


def neighbours():
    pix, y, z, x, core = place()

    def at(zz, xx, cc):
        return ((zz * 4 + xx) * 2 + cc, y)

    return dict(
        xr=at(z, step4(x, 1), core),
        xl=at(z, step4(x, 3), core),
        zr=at(step4(z, 1), x, core),
        zl=at(step4(z, 3), x, core),
        sib=at(z, x, 1 - core),
        yr=(pix, step4(y, 1)),
        yl=(pix, step4(y, 3)),
    )


def greet(names, near):
    barrier = pltpu.get_barrier_semaphore()
    for name in names:
        pl.semaphore_signal(barrier, inc=1, device_id=near[name], device_id_type=MESH)
    pl.semaphore_wait(barrier, len(names))


CHUNKS = 8


def pixel_kernel(
    cov, sk, gains, out, raw, om, gbuf, zf, zs, zb, got, csend,
    gsend, grecv, bsend, brecv, local,
):
    pix, y, z, x, core = place()
    near = neighbours()

    def load(i):
        return pltpu.make_async_copy(
            gains.at[pl.ds(8 * i, 8)], gbuf.at[pl.ds(8 * i, 8)], local.at[i]
        )

    mine = pltpu.make_async_copy(sk, raw.at[z, x, core], local.at[CHUNKS])
    mine.start()
    greet(("xr", "xl", "zr", "zl", "sib", "yr", "yl"), near)
    mine.wait()

    def send(k, ref, to):
        return pltpu.make_async_remote_copy(
            src_ref=ref, dst_ref=ref, send_sem=gsend.at[k], recv_sem=grecv.at[k],
            device_id=near[to], device_id_type=MESH,
        )

    lo, hi = pl.ds(0, 256), pl.ds(256, 256)
    a1 = raw.at[z, x, core, lo]
    b1 = raw.at[z, x, core, hi]
    cp = {}

    def go(k, ref, to):
        cp[k] = send(k, ref, to)
        cp[k].start()

    go(0, a1, "xr")
    go(1, a1, "xl")
    go(2, b1, "zr")
    go(3, b1, "zl")
    for i in range(CHUNKS):
        load(i).start()
    xm, xp, xo = step4(x, 3), step4(x, 1), step4(x, 2)
    zm, zp, zo = step4(z, 3), step4(z, 1), step4(z, 2)
    cp[0].wait_recv()
    go(4, raw.at[z, xm, core, pl.ds(0, 128)], "xr")
    cp[1].wait_recv()
    go(5, raw.at[z, xp, core, pl.ds(128, 128)], "xl")
    cp[2].wait_recv()
    go(6, raw.at[zm, x, core, pl.ds(256, 128)], "zr")
    cp[3].wait_recv()
    go(7, raw.at[zp, x, core, pl.ds(384, 128)], "zl")
    cp[4].wait_recv()
    cp[5].wait_recv()
    row = raw.at[z, :, core, lo]
    go(8, row, "zr")
    go(9, row, "zl")
    cp[6].wait_recv()
    cp[7].wait_recv()
    col = raw.at[:, x, core, hi]
    go(10, col, "xr")
    go(11, col, "xl")
    go(12, row, "sib")
    go(13, col, "sib")
    cp[8].wait_recv()
    go(14, raw.at[zm, pl.ds(0, 2), core, lo], "zr")
    cp[9].wait_recv()
    go(15, raw.at[zp, pl.ds(2, 2), core, lo], "zl")
    cp[10].wait_recv()
    go(16, raw.at[pl.ds(0, 2), xm, core, hi], "xr")
    cp[11].wait_recv()
    go(17, raw.at[pl.ds(2, 2), xp, core, hi], "xl")
    go(18, raw.at[zm, :, core, lo], "sib")
    go(19, raw.at[zp, :, core, lo], "sib")
    go(20, raw.at[:, xm, core, hi], "sib")
    go(21, raw.at[:, xp, core, hi], "sib")
    cp[14].wait_recv()
    cp[15].wait_recv()
    go(22, raw.at[zo, :, core, lo], "sib")
    cp[16].wait_recv()
    cp[17].wait_recv()
    go(23, raw.at[:, xo, core, hi], "sib")
    for k in (12, 13, 18, 19, 20, 21, 22, 23):
        cp[k].wait_recv()

    o = lax.broadcasted_iota(jnp.int32, (256, 256), 0)
    c = lax.broadcasted_iota(jnp.int32, (256, 256), 1)
    from_row = ((o % 64) // 4) * 16 + (o // 64) * 4 + o % 4
    swap = (c == from_row).astype(F32).astype(BF)

    @pl.loop(0, 32)
    def _(q):
        for g in range(2):
            part = raw[pl.ds(2 * g, 2), :, :, pl.ds(pl.multiple_of(16 * q, 16), 16), :]
            part = part.reshape(256, 256)
            turned = jnp.dot(swap, part, preferred_element_type=F32).astype(BF)
            om[pl.ds(4 * q, 4), pl.ds(64 * g, 64), :] = turned.reshape(4, 64, 256)

    c0, c1, c2, c3 = y, step4(y, 1), step4(y, 2), step4(y, 3)

    def rc(k, i, src, dst, to):
        return pltpu.make_async_remote_copy(
            src_ref=src, dst_ref=dst, send_sem=bsend.at[k, i], recv_sem=brecv.at[k, i],
            device_id=near[to], device_id_type=MESH,
        )

    def copies(i):
        t = 8 * i
        own = zb.at[pl.ds(t + 2 * c0, 2)]
        left = zb.at[t + 2 * c3]
        right = zb.at[t + 2 * c1 + 1]
        table = (
            (zs.at[t + 2 * c2], got.at[0, i], "yr"),
            (zs.at[t + 2 * c1 + 1], got.at[1, i], "yr"),
            (zs.at[t + 2 * c2 + 1], got.at[2, i], "yl"),
            (zs.at[t + 2 * c3], got.at[3, i], "yl"),
            (csend.at[0, i], got.at[4, i], "yr"),
            (csend.at[1, i], got.at[5, i], "yl"),
            (own, own, "yr"),
            (own, own, "yl"),
            (left, left, "yr"),
            (right, right, "yl"),
        )
        return lambda k: rc(k, i, *table[k])

    def store(i):
        return pltpu.make_async_copy(
            zb.at[pl.ds(8 * i, 8)], out.at[pl.ds(8 * i, 8)], local.at[CHUNKS + 1 + i]
        )

    @pl.loop(0, CHUNKS + 4)
    def _(tau):
        @pl.when(tau < CHUNKS)
        def _():
            load(tau).wait()

            @pl.loop(0, 8)
            def _(tt):
                t = tau * 8 + tt
                lhs = jnp.concatenate([gbuf[t, s] for s in range(8)], axis=1)
                rhs = jnp.concatenate([om[cov[t * 8 + s]] for s in range(8)], axis=0)
                acc = jnp.dot(lhs, rhs, preferred_element_type=F32)
                zf[t] = acc
                zs[t] = acc.astype(BF)

            m = copies(tau)
            for k in range(4):
                m(k).start()

        @pl.when(jnp.logical_and(tau >= 1, tau < CHUNKS + 1))
        def _():
            i = tau - 1
            m = copies(i)
            m(0).wait_recv()
            csend[0, i] = (got[0, i].astype(F32) + zf[8 * i + 2 * c1]).astype(BF)
            m(4).start()
            m(2).wait_recv()
            csend[1, i] = (got[2, i].astype(F32) + zf[8 * i + 2 * c3 + 1]).astype(BF)
            m(5).start()

        @pl.when(jnp.logical_and(tau >= 2, tau < CHUNKS + 2))
        def _():
            i = tau - 2
            m = copies(i)
            m(3).wait_recv()
            m(4).wait_recv()
            t = 8 * i + 2 * c0
            zb[t] = (zf[t] + got[3, i].astype(F32) + got[4, i].astype(F32)).astype(BF)
            m(1).wait_recv()
            m(5).wait_recv()
            zb[t + 1] = (zf[t + 1] + got[1, i].astype(F32) + got[5, i].astype(F32)).astype(BF)
            m(6).start()
            m(7).start()

        @pl.when(jnp.logical_and(tau >= 3, tau < CHUNKS + 3))
        def _():
            m = copies(tau - 3)
            m(6).wait_recv()
            m(8).start()
            m(7).wait_recv()
            m(9).start()

        @pl.when(tau >= 4)
        def _():
            m = copies(tau - 4)
            m(8).wait_recv()
            m(9).wait_recv()
            store(tau - 4).start()

    for k in range(24):
        cp[k].wait_send()

    @pl.loop(0, CHUNKS)
    def _(i):
        m = copies(i)
        for k in range(10):
            m(k).wait_send()
        store(i).wait()


def pixel_pass(sketch, gains, coverage):
    scratch = [
        pltpu.VMEM((4, 4, 2, 512, 256), BF),
        pltpu.VMEM((128, 128, 256), BF),
        pltpu.VMEM((64, 8, 128, 128), BF),
        pltpu.VMEM((64, 128, 256), F32),
        pltpu.VMEM((64, 128, 256), BF),
        pltpu.VMEM((64, 128, 256), BF),
        pltpu.VMEM((6, CHUNKS, 128, 256), BF),
        pltpu.VMEM((2, CHUNKS, 128, 256), BF),
        pltpu.SemaphoreType.DMA((24,)),
        pltpu.SemaphoreType.DMA((24,)),
        pltpu.SemaphoreType.DMA((10, CHUNKS)),
        pltpu.SemaphoreType.DMA((10, CHUNKS)),
        pltpu.SemaphoreType.DMA((2 * CHUNKS + 1,)),
    ]
    return pl.pallas_call(
        pixel_kernel,
        out_shape=jax.ShapeDtypeStruct((64, 128, 256), BF),
        in_specs=[
            pl.BlockSpec(memory_space=pltpu.SMEM),
            pl.BlockSpec(memory_space=pl.ANY),
            pl.BlockSpec(memory_space=pl.ANY),
        ],
        out_specs=pl.BlockSpec(memory_space=pl.ANY),
        scratch_shapes=scratch,
        compiler_params=pltpu.CompilerParams(
            collective_id=0, has_side_effects=True, vmem_limit_bytes=60 * MIB
        ),
        cost_estimate=pl.CostEstimate(
            flops=6_500_000_000, bytes_accessed=22_000_000, transcendentals=0
        ),
        name="pixel_pass",
    )(coverage.reshape(-1), sketch.reshape(512, 256), gains)


TILES_STEP = 4


def beam_kernel(cov, g, zb, out, acc, split, sems):
    step = pl.program_id(0)

    @pl.when(step == 0)
    def _():
        @pl.loop(0, 128)
        def _(b):
            acc[b] = jnp.zeros((128, 256), F32)

    for tt in range(TILES_STEP):
        rows = zb[tt]
        for s in range(8):
            b = cov[(step * TILES_STEP + tt) * 8 + s]
            acc[b] += lax.dot_general(
                g[tt, s], rows, (((0,), (0,)), ((), ())), preferred_element_type=F32
            )

    @pl.when(step == pl.num_programs(0) - 1)
    def _():
        low = lax.broadcasted_iota(jnp.int32, (16, 8, 256), 1) < 4

        def store(i):
            return pltpu.make_async_copy(
                split.at[:, :, pl.ds(pl.multiple_of(64 * i, 64), 64)],
                out.at[:, :, pl.ds(pl.multiple_of(64 * i, 64), 64)],
                sems.at[i],
            )

        @pl.loop(0, 8)
        def _(i):
            @pl.loop(0, 8)
            def _(j):
                pair = i * 8 + j
                a = acc[2 * pair].reshape(16, 8, 256)
                b = acc[2 * pair + 1].reshape(16, 8, 256)
                at = pl.ds(pl.multiple_of(8 * pair, 8), 8)
                split[:, 0, at, :] = jnp.where(low, a, pltpu.roll(b, 4, 1))
                split[:, 1, at, :] = jnp.where(low, pltpu.roll(a, 4, 1), b)

            store(i).start()

        @pl.loop(0, 8)
        def _(i):
            store(i).wait()


def beam_pass(coverage, gains, rounded):
    spec = pltpu.PrefetchScalarGridSpec(
        num_scalar_prefetch=1,
        grid=(64 // TILES_STEP,),
        in_specs=[
            pl.BlockSpec((TILES_STEP, 8, 128, 128), lambda i, c: (i, 0, 0, 0)),
            pl.BlockSpec((TILES_STEP, 128, 256), lambda i, c: (i, 0, 0)),
        ],
        out_specs=pl.BlockSpec(memory_space=pl.ANY),
        scratch_shapes=[
            pltpu.VMEM((128, 128, 256), F32),
            pltpu.VMEM((16, 2, 512, 256), F32),
            pltpu.SemaphoreType.DMA((8,)),
        ],
    )
    return pl.pallas_call(
        beam_kernel,
        grid_spec=spec,
        out_shape=jax.ShapeDtypeStruct((16, 2, 512, 256), F32),
        compiler_params=pltpu.CompilerParams(vmem_limit_bytes=56 * MIB),
        cost_estimate=pl.CostEstimate(
            flops=4_300_000_000, bytes_accessed=38_000_000, transcendentals=0
        ),
        name="beam_pass",
    )(coverage.reshape(-1), gains, rounded)


def local(sketch, gains, coverage):
    rounded = pixel_pass(sketch, gains, coverage)
    total = beam_pass(coverage, gains, rounded)
    flat = lax.psum_scatter(
        total.reshape(32, 512, 256), "pix", scatter_dimension=0, tiled=False
    )
    local_gram = jnp.dot(
        flat.T, flat, precision=lax.Precision.HIGHEST, preferred_element_type=F32
    )
    gram = lax.psum(local_gram, ("pix", "beam"))
    lower = jnp.linalg.cholesky(gram)
    solved = jax.scipy.linalg.solve_triangular(lower, flat.T, lower=True).T
    scale = jnp.sqrt(jnp.float32(BEAMS))
    return ((solved * scale).reshape(sketch.shape), lower.T / scale)


def solution(mesh):
    return jax.shard_map(
        local,
        mesh=mesh,
        in_specs=(P("beam", "pix", None), P("pix", "beam", None, None), P("pix", "beam")),
        out_specs=(P("beam", "pix", None), P()),
        check_vma=False,
    )
```

```python
import functools

import jax
import jax.numpy as jnp
from jax import lax
from jax.experimental import pallas as pl
from jax.experimental.pallas import tpu as pltpu
from jax.sharding import PartitionSpec as P

BEAMS = 65536
BF = jnp.bfloat16
F32 = jnp.float32
MESH = pl.DeviceIdType.MESH
MIB = 1 << 20


def place():
    pix = lax.axis_index("pix")
    y = lax.axis_index("beam")
    core = lax.rem(pix, 2)
    x = lax.rem(lax.div(pix, 2), 4)
    z = lax.div(pix, 8)
    return pix, y, z, x, core


def step4(v, d):
    return lax.rem(v + d, 4)


def neighbours():
    pix, y, z, x, core = place()

    def at(zz, xx, cc):
        return ((zz * 4 + xx) * 2 + cc, y)

    return dict(
        xr=at(z, step4(x, 1), core),
        xl=at(z, step4(x, 3), core),
        zr=at(step4(z, 1), x, core),
        zl=at(step4(z, 3), x, core),
        sib=at(z, x, 1 - core),
        yr=(pix, step4(y, 1)),
        yl=(pix, step4(y, 3)),
        xo=at(z, step4(x, 2), core),
        zo=at(step4(z, 2), x, core),
        yo=(pix, step4(y, 2)),
    )


def greet(names, near):
    barrier = pltpu.get_barrier_semaphore()
    for name in names:
        pl.semaphore_signal(barrier, inc=1, device_id=near[name], device_id_type=MESH)
    pl.semaphore_wait(barrier, len(names))


CHUNKS = 8


def pixel_kernel(
    cov, sk, gains, out, raw, om, gbuf, zf, zs, zb, got, csend,
    gsend, grecv, bsend, brecv, local,
):
    pix, y, z, x, core = place()
    near = neighbours()

    def load(i):
        return pltpu.make_async_copy(
            gains.at[pl.ds(8 * i, 8)], gbuf.at[pl.ds(8 * i, 8)], local.at[i]
        )

    mine = pltpu.make_async_copy(sk, raw.at[z, x, core], local.at[CHUNKS])
    mine.start()
    greet(("xr", "xl", "zr", "zl", "sib", "yr", "yl"), near)
    mine.wait()

    def send(k, ref, to):
        return pltpu.make_async_remote_copy(
            src_ref=ref, dst_ref=ref, send_sem=gsend.at[k], recv_sem=grecv.at[k],
            device_id=near[to], device_id_type=MESH,
        )

    lo, hi = pl.ds(0, 256), pl.ds(256, 256)
    a1 = raw.at[z, x, core, lo]
    b1 = raw.at[z, x, core, hi]
    cp = {}

    def go(k, ref, to):
        cp[k] = send(k, ref, to)
        cp[k].start()

    go(0, a1, "xr")
    go(1, a1, "xl")
    go(2, b1, "zr")
    go(3, b1, "zl")
    for i in range(CHUNKS):
        load(i).start()
    xm, xp, xo = step4(x, 3), step4(x, 1), step4(x, 2)
    zm, zp, zo = step4(z, 3), step4(z, 1), step4(z, 2)
    cp[0].wait_recv()
    go(4, raw.at[z, xm, core, pl.ds(0, 128)], "xr")
    cp[1].wait_recv()
    go(5, raw.at[z, xp, core, pl.ds(128, 128)], "xl")
    cp[2].wait_recv()
    go(6, raw.at[zm, x, core, pl.ds(256, 128)], "zr")
    cp[3].wait_recv()
    go(7, raw.at[zp, x, core, pl.ds(384, 128)], "zl")
    cp[4].wait_recv()
    cp[5].wait_recv()
    row = raw.at[z, :, core, lo]
    go(8, row, "zr")
    go(9, row, "zl")
    cp[6].wait_recv()
    cp[7].wait_recv()
    col = raw.at[:, x, core, hi]
    go(10, col, "xr")
    go(11, col, "xl")
    go(12, row, "sib")
    go(13, col, "sib")
    cp[8].wait_recv()
    go(14, raw.at[zm, pl.ds(0, 2), core, lo], "zr")
    cp[9].wait_recv()
    go(15, raw.at[zp, pl.ds(2, 2), core, lo], "zl")
    cp[10].wait_recv()
    go(16, raw.at[pl.ds(0, 2), xm, core, hi], "xr")
    cp[11].wait_recv()
    go(17, raw.at[pl.ds(2, 2), xp, core, hi], "xl")
    go(18, raw.at[zm, :, core, lo], "sib")
    go(19, raw.at[zp, :, core, lo], "sib")
    go(20, raw.at[:, xm, core, hi], "sib")
    go(21, raw.at[:, xp, core, hi], "sib")
    cp[14].wait_recv()
    cp[15].wait_recv()
    go(22, raw.at[zo, :, core, lo], "sib")
    cp[16].wait_recv()
    cp[17].wait_recv()
    go(23, raw.at[:, xo, core, hi], "sib")
    for k in (12, 13, 18, 19, 20, 21, 22, 23):
        cp[k].wait_recv()

    o = lax.broadcasted_iota(jnp.int32, (256, 256), 0)
    c = lax.broadcasted_iota(jnp.int32, (256, 256), 1)
    from_row = ((o % 64) // 4) * 16 + (o // 64) * 4 + o % 4
    swap = (c == from_row).astype(F32).astype(BF)

    @pl.loop(0, 32)
    def _(q):
        for g in range(2):
            part = raw[pl.ds(2 * g, 2), :, :, pl.ds(pl.multiple_of(16 * q, 16), 16), :]
            part = part.reshape(256, 256)
            turned = jnp.dot(swap, part, preferred_element_type=F32).astype(BF)
            om[pl.ds(4 * q, 4), pl.ds(64 * g, 64), :] = turned.reshape(4, 64, 256)

    c0, c1, c2, c3 = y, step4(y, 1), step4(y, 2), step4(y, 3)

    def rc(k, i, src, dst, to):
        return pltpu.make_async_remote_copy(
            src_ref=src, dst_ref=dst, send_sem=bsend.at[k, i], recv_sem=brecv.at[k, i],
            device_id=near[to], device_id_type=MESH,
        )

    def copies(i):
        t = 8 * i
        own = zb.at[pl.ds(t + 2 * c0, 2)]
        left = zb.at[t + 2 * c3]
        right = zb.at[t + 2 * c1 + 1]
        table = (
            (zs.at[t + 2 * c2], got.at[0, i], "yr"),
            (zs.at[t + 2 * c1 + 1], got.at[1, i], "yr"),
            (zs.at[t + 2 * c2 + 1], got.at[2, i], "yl"),
            (zs.at[t + 2 * c3], got.at[3, i], "yl"),
            (csend.at[0, i], got.at[4, i], "yr"),
            (csend.at[1, i], got.at[5, i], "yl"),
            (own, own, "yr"),
            (own, own, "yl"),
            (left, left, "yr"),
            (right, right, "yl"),
        )
        return lambda k: rc(k, i, *table[k])

    def store(i):
        return pltpu.make_async_copy(
            zb.at[pl.ds(8 * i, 8)], out.at[pl.ds(8 * i, 8)], local.at[CHUNKS + 1 + i]
        )

    @pl.loop(0, CHUNKS + 4)
    def _(tau):
        @pl.when(tau < CHUNKS)
        def _():
            load(tau).wait()

            @pl.loop(0, 8)
            def _(tt):
                t = tau * 8 + tt
                lhs = jnp.concatenate([gbuf[t, s] for s in range(8)], axis=1)
                rhs = jnp.concatenate([om[cov[t * 8 + s]] for s in range(8)], axis=0)
                acc = jnp.dot(lhs, rhs, preferred_element_type=F32)
                zf[t] = acc
                zs[t] = acc.astype(BF)

            m = copies(tau)
            for k in range(4):
                m(k).start()

        @pl.when(jnp.logical_and(tau >= 1, tau < CHUNKS + 1))
        def _():
            i = tau - 1
            m = copies(i)
            m(0).wait_recv()
            csend[0, i] = (got[0, i].astype(F32) + zf[8 * i + 2 * c1]).astype(BF)
            m(4).start()
            m(2).wait_recv()
            csend[1, i] = (got[2, i].astype(F32) + zf[8 * i + 2 * c3 + 1]).astype(BF)
            m(5).start()

        @pl.when(jnp.logical_and(tau >= 2, tau < CHUNKS + 2))
        def _():
            i = tau - 2
            m = copies(i)
            m(3).wait_recv()
            m(4).wait_recv()
            t = 8 * i + 2 * c0
            zb[t] = (zf[t] + got[3, i].astype(F32) + got[4, i].astype(F32)).astype(BF)
            m(1).wait_recv()
            m(5).wait_recv()
            zb[t + 1] = (zf[t + 1] + got[1, i].astype(F32) + got[5, i].astype(F32)).astype(BF)
            m(6).start()
            m(7).start()

        @pl.when(jnp.logical_and(tau >= 3, tau < CHUNKS + 3))
        def _():
            m = copies(tau - 3)
            m(6).wait_recv()
            m(8).start()
            m(7).wait_recv()
            m(9).start()

        @pl.when(tau >= 4)
        def _():
            m = copies(tau - 4)
            m(8).wait_recv()
            m(9).wait_recv()
            store(tau - 4).start()

    for k in range(24):
        cp[k].wait_send()

    @pl.loop(0, CHUNKS)
    def _(i):
        m = copies(i)
        for k in range(10):
            m(k).wait_send()
        store(i).wait()


def pixel_pass(sketch, gains, coverage):
    scratch = [
        pltpu.VMEM((4, 4, 2, 512, 256), BF),
        pltpu.VMEM((128, 128, 256), BF),
        pltpu.VMEM((64, 8, 128, 128), BF),
        pltpu.VMEM((64, 128, 256), F32),
        pltpu.VMEM((64, 128, 256), BF),
        pltpu.VMEM((64, 128, 256), BF),
        pltpu.VMEM((6, CHUNKS, 128, 256), BF),
        pltpu.VMEM((2, CHUNKS, 128, 256), BF),
        pltpu.SemaphoreType.DMA((24,)),
        pltpu.SemaphoreType.DMA((24,)),
        pltpu.SemaphoreType.DMA((10, CHUNKS)),
        pltpu.SemaphoreType.DMA((10, CHUNKS)),
        pltpu.SemaphoreType.DMA((2 * CHUNKS + 1,)),
    ]
    return pl.pallas_call(
        pixel_kernel,
        out_shape=jax.ShapeDtypeStruct((64, 128, 256), BF),
        in_specs=[
            pl.BlockSpec(memory_space=pltpu.SMEM),
            pl.BlockSpec(memory_space=pl.ANY),
            pl.BlockSpec(memory_space=pl.ANY),
        ],
        out_specs=pl.BlockSpec(memory_space=pl.ANY),
        scratch_shapes=scratch,
        compiler_params=pltpu.CompilerParams(
            collective_id=0, has_side_effects=True, vmem_limit_bytes=60 * MIB
        ),
        cost_estimate=pl.CostEstimate(
            flops=6_500_000_000, bytes_accessed=22_000_000, transcendentals=0
        ),
        name="pixel_pass",
    )(coverage.reshape(-1), sketch.reshape(512, 256), gains)


TILES_STEP = 4


def beam_kernel(cov, g, zb, out, acc, split, sems):
    step = pl.program_id(0)

    @pl.when(step == 0)
    def _():
        @pl.loop(0, 128)
        def _(b):
            acc[b] = jnp.zeros((128, 256), F32)

    for tt in range(TILES_STEP):
        rows = zb[tt]
        for s in range(8):
            b = cov[(step * TILES_STEP + tt) * 8 + s]
            acc[b] += lax.dot_general(
                g[tt, s], rows, (((0,), (0,)), ((), ())), preferred_element_type=F32
            )

    @pl.when(step == pl.num_programs(0) - 1)
    def _():
        low = lax.broadcasted_iota(jnp.int32, (16, 8, 256), 1) < 4

        def store(i):
            return pltpu.make_async_copy(
                split.at[:, :, pl.ds(pl.multiple_of(64 * i, 64), 64)],
                out.at[:, :, pl.ds(pl.multiple_of(64 * i, 64), 64)],
                sems.at[i],
            )

        @pl.loop(0, 8)
        def _(i):
            @pl.loop(0, 8)
            def _(j):
                pair = i * 8 + j
                a = acc[2 * pair].reshape(16, 8, 256)
                b = acc[2 * pair + 1].reshape(16, 8, 256)
                at = pl.ds(pl.multiple_of(8 * pair, 8), 8)
                split[:, 0, at, :] = jnp.where(low, a, pltpu.roll(b, 4, 1))
                split[:, 1, at, :] = jnp.where(low, pltpu.roll(a, 4, 1), b)

            store(i).start()

        @pl.loop(0, 8)
        def _(i):
            store(i).wait()


def beam_pass(coverage, gains, rounded):
    spec = pltpu.PrefetchScalarGridSpec(
        num_scalar_prefetch=1,
        grid=(64 // TILES_STEP,),
        in_specs=[
            pl.BlockSpec((TILES_STEP, 8, 128, 128), lambda i, c: (i, 0, 0, 0)),
            pl.BlockSpec((TILES_STEP, 128, 256), lambda i, c: (i, 0, 0)),
        ],
        out_specs=pl.BlockSpec(memory_space=pl.ANY),
        scratch_shapes=[
            pltpu.VMEM((128, 128, 256), F32),
            pltpu.VMEM((16, 2, 512, 256), F32),
            pltpu.SemaphoreType.DMA((8,)),
        ],
    )
    return pl.pallas_call(
        beam_kernel,
        grid_spec=spec,
        out_shape=jax.ShapeDtypeStruct((16, 2, 512, 256), F32),
        compiler_params=pltpu.CompilerParams(vmem_limit_bytes=56 * MIB),
        cost_estimate=pl.CostEstimate(
            flops=4_300_000_000, bytes_accessed=38_000_000, transcendentals=0
        ),
        name="beam_pass",
    )(coverage.reshape(-1), gains, rounded)

SUB = 4
ROWS = 256 // SUB
HALF = ROWS // 2


def sum_kernel(
    part, flat, gram, own, sib, got1, got2, gacc, gout, gsib, gx, gz, gy,
    csend, crecv, rsend, rrecv, gsend, grecv, local,
):
    pix, y, z, x, core = place()
    near = neighbours()
    other = 1 - core

    def rows(h, j):
        return pl.ds(pl.multiple_of(256 * h + ROWS * j, ROWS), ROWS)

    def load(h, j):
        return pltpu.make_async_copy(
            part.at[:, :, core, rows(h, j)], own.at[h, j], local.at[h, j]
        )

    def swap(h, j):
        return pltpu.make_async_remote_copy(
            src_ref=part.at[:, :, other, rows(h, j)], dst_ref=sib.at[h, j],
            send_sem=csend.at[h, j], recv_sem=crecv.at[h, j],
            device_id=near["sib"], device_id_type=MESH,
        )

    for j in range(SUB):
        for h in range(2):
            load(h, j).start()
    greet(("xr", "xl", "zr", "zl", "sib", "yr", "yl", "xo", "zo", "yo"), near)
    for j in range(SUB):
        for h in range(2):
            swap(h, j).start()

    def ring(h, phase):
        if (h == 0) == (phase == 0):
            return x, "xr", "xl"
        return z, "zr", "zl"

    def piece(h, j, phase, d, lo):
        if phase == 0:
            two = pl.ds(0 if lo else 2, 2)
            return own.at[h, j, two, d] if h == 0 else own.at[h, j, d, two]
        n = pl.ds(0 if lo else HALF, HALF)
        return own.at[h, j, d, x, n] if h == 0 else own.at[h, j, z, d, n]

    def msg(h, j, phase, k):
        c, right, left = ring(h, phase)
        got = got1 if phase == 0 else got2
        d, lo, to = (
            (step4(c, 2), True, right),
            (step4(c, 1), False, right),
            (step4(c, 2), False, left),
            (step4(c, 3), True, left),
            (step4(c, 1), True, right),
            (step4(c, 3), False, left),
        )[k]
        return pltpu.make_async_remote_copy(
            src_ref=piece(h, j, phase, d, lo), dst_ref=got.at[h, j, k],
            send_sem=rsend.at[h, j, phase, k], recv_sem=rrecv.at[h, j, phase, k],
            device_id=near[to], device_id_type=MESH,
        )

    def first(h, j, phase):
        for k in range(4):
            msg(h, j, phase, k).start()

    def second(h, j, phase):
        c = ring(h, phase)[0]
        got = got1 if phase == 0 else got2
        msg(h, j, phase, 0).wait_recv()
        mid = piece(h, j, phase, step4(c, 1), True)
        mid[...] += got[h, j, 0]
        msg(h, j, phase, 4).start()
        msg(h, j, phase, 2).wait_recv()
        mid = piece(h, j, phase, step4(c, 3), False)
        mid[...] += got[h, j, 2]
        msg(h, j, phase, 5).start()

    def finish(h, j, phase):
        c = ring(h, phase)[0]
        got = got1 if phase == 0 else got2
        for k in (3, 4, 1, 5):
            msg(h, j, phase, k).wait_recv()
        lo = piece(h, j, phase, c, True)
        lo[...] += got[h, j, 3] + got[h, j, 4]
        hi = piece(h, j, phase, c, False)
        hi[...] += got[h, j, 1] + got[h, j, 5]

    def stage(tau, after, work):
        @pl.when(jnp.logical_and(tau >= after, tau < after + SUB))
        def _():
            for h in range(2):
                work(h, tau - after)

    @pl.loop(0, SUB + 4)
    def _(tau):
        def begin(h, j):
            load(h, j).wait()
            swap(h, j).wait_recv()

            @pl.loop(0, 4)
            def _(i):
                own[h, j, i] += sib[h, j, i]

            first(h, j, 0)

        def turn(h, j):
            finish(h, j, 0)
            first(h, j, 1)

        def end(h, j):
            finish(h, j, 1)
            flat[rows(h, j), :] = own[h, j, z, x]

        stage(tau, 0, begin)
        stage(tau, 1, lambda h, j: second(h, j, 0))
        stage(tau, 2, turn)
        stage(tau, 3, lambda h, j: second(h, j, 1))
        stage(tau, 4, end)

    f = flat[...]
    gacc[...] = lax.dot_general(
        f, f, (((0,), (0,)), ((), ())),
        precision=lax.Precision.HIGHEST, preferred_element_type=F32,
    )

    def gmsg(k, src, dst, to):
        return pltpu.make_async_remote_copy(
            src_ref=src, dst_ref=dst, send_sem=gsend.at[k], recv_sem=grecv.at[k],
            device_id=near[to], device_id_type=MESH,
        )

    def block(at, n, ref=gacc):
        return ref.at[pl.ds(pl.multiple_of(at, n), n)]

    sent = []

    def exchange(k, pairs):
        todo = [gmsg(k + n, *p) for n, p in enumerate(pairs)]
        for m in todo:
            m.start()
        for m in todo:
            m.wait_recv()
        sent.extend(todo)

    base = 128 * core
    exchange(0, [(block(128 * other, 128), gsib, "sib")])
    mine = block(base, 128)
    mine[...] += gsib[...]
    xat = base + 32 * x
    exchange(1, [
        (block(base + 32 * step4(x, d), 32), gx.at[d - 1], to)
        for d, to in ((1, "xr"), (2, "xo"), (3, "xl"))
    ])
    mine = block(xat, 32)
    mine[...] += gx[0] + gx[1] + gx[2]
    zat = xat + 8 * z
    exchange(4, [
        (block(xat + 8 * step4(z, d), 8), gz.at[d - 1], to)
        for d, to in ((1, "zr"), (2, "zo"), (3, "zl"))
    ])
    mine = block(zat, 8)
    gy[y] = mine[...] + (gz[0] + gz[1] + gz[2])
    exchange(7, [(gy.at[y], gy.at[y], to) for to in ("yr", "yo", "yl")])
    mine = block(zat, 8, gout)
    mine[...] = (gy[0] + gy[1]) + (gy[2] + gy[3])
    exchange(10, [(mine, mine, to) for to in ("zr", "zo", "zl")])
    mine = block(xat, 32, gout)
    exchange(13, [(mine, mine, to) for to in ("xr", "xo", "xl")])
    mine = block(base, 128, gout)
    exchange(16, [(mine, mine, "sib")])
    gram[...] = gout[...]
    for m in sent:
        m.wait_send()

    @pl.loop(0, SUB)
    def _(j):
        for h in range(2):
            swap(h, j).wait_send()
            for phase in range(2):
                for k in range(6):
                    msg(h, j, phase, k).wait_send()


def sum_pass(total):
    scratch = [
        pltpu.VMEM((2, SUB, 4, 4, ROWS, 256), F32),
        pltpu.VMEM((2, SUB, 4, 4, ROWS, 256), F32),
        pltpu.VMEM((2, SUB, 6, 2, ROWS, 256), F32),
        pltpu.VMEM((2, SUB, 6, HALF, 256), F32),
        pltpu.VMEM((256, 256), F32),
        pltpu.VMEM((256, 256), F32),
        pltpu.VMEM((128, 256), F32),
        pltpu.VMEM((3, 32, 256), F32),
        pltpu.VMEM((3, 8, 256), F32),
        pltpu.VMEM((4, 8, 256), F32),
        pltpu.SemaphoreType.DMA((2, SUB)),
        pltpu.SemaphoreType.DMA((2, SUB)),
        pltpu.SemaphoreType.DMA((2, SUB, 2, 6)),
        pltpu.SemaphoreType.DMA((2, SUB, 2, 6)),
        pltpu.SemaphoreType.DMA((17,)),
        pltpu.SemaphoreType.DMA((17,)),
        pltpu.SemaphoreType.DMA((2, SUB)),
    ]
    return pl.pallas_call(
        sum_kernel,
        out_shape=(
            jax.ShapeDtypeStruct((512, 256), F32),
            jax.ShapeDtypeStruct((256, 256), F32),
        ),
        in_specs=[pl.BlockSpec(memory_space=pl.ANY)],
        out_specs=(
            pl.BlockSpec(memory_space=pltpu.VMEM),
            pl.BlockSpec(memory_space=pltpu.VMEM),
        ),
        scratch_shapes=scratch,
        compiler_params=pltpu.CompilerParams(
            collective_id=1, has_side_effects=True, vmem_limit_bytes=48 * MIB
        ),
        cost_estimate=pl.CostEstimate(
            flops=500_000_000, bytes_accessed=18_000_000, transcendentals=0
        ),
        name="sum_pass",
    )(total)


def local(sketch, gains, coverage):
    rounded = pixel_pass(sketch, gains, coverage)
    total = beam_pass(coverage, gains, rounded)
    flat, gram = sum_pass(total.reshape(4, 4, 2, 512, 256))
    lower = jnp.linalg.cholesky(gram)
    solved = jax.scipy.linalg.solve_triangular(lower, flat.T, lower=True).T
    scale = jnp.sqrt(jnp.float32(BEAMS))
    return ((solved * scale).reshape(sketch.shape), lower.T / scale)


def solution(mesh):
    return jax.shard_map(
        local,
        mesh=mesh,
        in_specs=(P("beam", "pix", None), P("pix", "beam", None, None), P("pix", "beam")),
        out_specs=(P("beam", "pix", None), P()),
        check_vma=False,
    )
```

```python
import functools

import jax
import jax.numpy as jnp
from jax import lax
from jax.experimental import pallas as pl
from jax.experimental.pallas import tpu as pltpu
from jax.sharding import PartitionSpec as P

BEAMS = 65536
BF = jnp.bfloat16
F32 = jnp.float32
MESH = pl.DeviceIdType.MESH
MIB = 1 << 20


def place():
    pix = lax.axis_index("pix")
    y = lax.axis_index("beam")
    core = lax.rem(pix, 2)
    x = lax.rem(lax.div(pix, 2), 4)
    z = lax.div(pix, 8)
    return pix, y, z, x, core


def step4(v, d):
    return lax.rem(v + d, 4)


def neighbours():
    pix, y, z, x, core = place()

    def at(zz, xx, cc):
        return ((zz * 4 + xx) * 2 + cc, y)

    return dict(
        xr=at(z, step4(x, 1), core),
        xl=at(z, step4(x, 3), core),
        zr=at(step4(z, 1), x, core),
        zl=at(step4(z, 3), x, core),
        sib=at(z, x, 1 - core),
        yr=(pix, step4(y, 1)),
        yl=(pix, step4(y, 3)),
        xo=at(z, step4(x, 2), core),
        zo=at(step4(z, 2), x, core),
        yo=(pix, step4(y, 2)),
    )


def greet(names, near):
    barrier = pltpu.get_barrier_semaphore()
    for name in names:
        pl.semaphore_signal(barrier, inc=1, device_id=near[name], device_id_type=MESH)
    pl.semaphore_wait(barrier, len(names))


CHUNKS = 8


def pixel_kernel(
    cov, sk, gains, out, raw, om, gbuf, zf, zs, zb, got, csend,
    gsend, grecv, bsend, brecv, local,
):
    pix, y, z, x, core = place()
    near = neighbours()

    def load(i):
        return pltpu.make_async_copy(
            gains.at[pl.ds(8 * i, 8)], gbuf.at[pl.ds(8 * i, 8)], local.at[i]
        )

    mine = pltpu.make_async_copy(sk, raw.at[z, x, core], local.at[CHUNKS])
    mine.start()
    greet(("xr", "xl", "zr", "zl", "sib", "yr", "yl"), near)
    mine.wait()

    def send(k, ref, to):
        return pltpu.make_async_remote_copy(
            src_ref=ref, dst_ref=ref, send_sem=gsend.at[k], recv_sem=grecv.at[k],
            device_id=near[to], device_id_type=MESH,
        )

    lo, hi = pl.ds(0, 256), pl.ds(256, 256)
    a1 = raw.at[z, x, core, lo]
    b1 = raw.at[z, x, core, hi]
    cp = {}

    def go(k, ref, to):
        cp[k] = send(k, ref, to)
        cp[k].start()

    go(0, a1, "xr")
    go(1, a1, "xl")
    go(2, b1, "zr")
    go(3, b1, "zl")
    for i in range(CHUNKS):
        load(i).start()
    xm, xp, xo = step4(x, 3), step4(x, 1), step4(x, 2)
    zm, zp, zo = step4(z, 3), step4(z, 1), step4(z, 2)
    cp[0].wait_recv()
    go(4, raw.at[z, xm, core, pl.ds(0, 128)], "xr")
    cp[1].wait_recv()
    go(5, raw.at[z, xp, core, pl.ds(128, 128)], "xl")
    cp[2].wait_recv()
    go(6, raw.at[zm, x, core, pl.ds(256, 128)], "zr")
    cp[3].wait_recv()
    go(7, raw.at[zp, x, core, pl.ds(384, 128)], "zl")
    cp[4].wait_recv()
    cp[5].wait_recv()
    row = raw.at[z, :, core, lo]
    go(8, row, "zr")
    go(9, row, "zl")
    cp[6].wait_recv()
    cp[7].wait_recv()
    col = raw.at[:, x, core, hi]
    go(10, col, "xr")
    go(11, col, "xl")
    go(12, row, "sib")
    go(13, col, "sib")
    cp[8].wait_recv()
    go(14, raw.at[zm, pl.ds(0, 2), core, lo], "zr")
    cp[9].wait_recv()
    go(15, raw.at[zp, pl.ds(2, 2), core, lo], "zl")
    cp[10].wait_recv()
    go(16, raw.at[pl.ds(0, 2), xm, core, hi], "xr")
    cp[11].wait_recv()
    go(17, raw.at[pl.ds(2, 2), xp, core, hi], "xl")
    go(18, raw.at[zm, :, core, lo], "sib")
    go(19, raw.at[zp, :, core, lo], "sib")
    go(20, raw.at[:, xm, core, hi], "sib")
    go(21, raw.at[:, xp, core, hi], "sib")
    cp[14].wait_recv()
    cp[15].wait_recv()
    go(22, raw.at[zo, :, core, lo], "sib")
    cp[16].wait_recv()
    cp[17].wait_recv()
    go(23, raw.at[:, xo, core, hi], "sib")
    for k in (12, 13, 18, 19, 20, 21, 22, 23):
        cp[k].wait_recv()

    o = lax.broadcasted_iota(jnp.int32, (256, 256), 0)
    c = lax.broadcasted_iota(jnp.int32, (256, 256), 1)
    from_row = ((o % 64) // 4) * 16 + (o // 64) * 4 + o % 4
    swap = (c == from_row).astype(F32).astype(BF)

    @pl.loop(0, 32)
    def _(q):
        for g in range(2):
            part = raw[pl.ds(2 * g, 2), :, :, pl.ds(pl.multiple_of(16 * q, 16), 16), :]
            part = part.reshape(256, 256)
            turned = jnp.dot(swap, part, preferred_element_type=F32).astype(BF)
            om[pl.ds(4 * q, 4), pl.ds(64 * g, 64), :] = turned.reshape(4, 64, 256)

    c0, c1, c2, c3 = y, step4(y, 1), step4(y, 2), step4(y, 3)

    def rc(k, i, src, dst, to):
        return pltpu.make_async_remote_copy(
            src_ref=src, dst_ref=dst, send_sem=bsend.at[k, i], recv_sem=brecv.at[k, i],
            device_id=near[to], device_id_type=MESH,
        )

    def copies(i):
        t = 8 * i
        own = zb.at[pl.ds(t + 2 * c0, 2)]
        left = zb.at[t + 2 * c3]
        right = zb.at[t + 2 * c1 + 1]
        table = (
            (zs.at[t + 2 * c2], got.at[0, i], "yr"),
            (zs.at[t + 2 * c1 + 1], got.at[1, i], "yr"),
            (zs.at[t + 2 * c2 + 1], got.at[2, i], "yl"),
            (zs.at[t + 2 * c3], got.at[3, i], "yl"),
            (csend.at[0, i], got.at[4, i], "yr"),
            (csend.at[1, i], got.at[5, i], "yl"),
            (own, own, "yr"),
            (own, own, "yl"),
            (left, left, "yr"),
            (right, right, "yl"),
        )
        return lambda k: rc(k, i, *table[k])

    def store(i):
        return pltpu.make_async_copy(
            zb.at[pl.ds(8 * i, 8)], out.at[pl.ds(8 * i, 8)], local.at[CHUNKS + 1 + i]
        )

    @pl.loop(0, CHUNKS + 4)
    def _(tau):
        @pl.when(tau < CHUNKS)
        def _():
            load(tau).wait()

            @pl.loop(0, 8)
            def _(tt):
                t = tau * 8 + tt
                lhs = jnp.concatenate([gbuf[t, s] for s in range(8)], axis=1)
                rhs = jnp.concatenate([om[cov[t * 8 + s]] for s in range(8)], axis=0)
                acc = jnp.dot(lhs, rhs, preferred_element_type=F32)
                zf[t] = acc
                zs[t] = acc.astype(BF)

            m = copies(tau)
            for k in range(4):
                m(k).start()

        @pl.when(jnp.logical_and(tau >= 1, tau < CHUNKS + 1))
        def _():
            i = tau - 1
            m = copies(i)
            m(0).wait_recv()
            csend[0, i] = (got[0, i].astype(F32) + zf[8 * i + 2 * c1]).astype(BF)
            m(4).start()
            m(2).wait_recv()
            csend[1, i] = (got[2, i].astype(F32) + zf[8 * i + 2 * c3 + 1]).astype(BF)
            m(5).start()

        @pl.when(jnp.logical_and(tau >= 2, tau < CHUNKS + 2))
        def _():
            i = tau - 2
            m = copies(i)
            m(3).wait_recv()
            m(4).wait_recv()
            t = 8 * i + 2 * c0
            zb[t] = (zf[t] + got[3, i].astype(F32) + got[4, i].astype(F32)).astype(BF)
            m(1).wait_recv()
            m(5).wait_recv()
            zb[t + 1] = (zf[t + 1] + got[1, i].astype(F32) + got[5, i].astype(F32)).astype(BF)
            m(6).start()
            m(7).start()

        @pl.when(jnp.logical_and(tau >= 3, tau < CHUNKS + 3))
        def _():
            m = copies(tau - 3)
            m(6).wait_recv()
            m(8).start()
            m(7).wait_recv()
            m(9).start()

        @pl.when(tau >= 4)
        def _():
            m = copies(tau - 4)
            m(8).wait_recv()
            m(9).wait_recv()
            store(tau - 4).start()

    for k in range(24):
        cp[k].wait_send()

    @pl.loop(0, CHUNKS)
    def _(i):
        m = copies(i)
        for k in range(10):
            m(k).wait_send()
        store(i).wait()


def pixel_pass(sketch, gains, coverage):
    scratch = [
        pltpu.VMEM((4, 4, 2, 512, 256), BF),
        pltpu.VMEM((128, 128, 256), BF),
        pltpu.VMEM((64, 8, 128, 128), BF),
        pltpu.VMEM((64, 128, 256), F32),
        pltpu.VMEM((64, 128, 256), BF),
        pltpu.VMEM((64, 128, 256), BF),
        pltpu.VMEM((6, CHUNKS, 128, 256), BF),
        pltpu.VMEM((2, CHUNKS, 128, 256), BF),
        pltpu.SemaphoreType.DMA((24,)),
        pltpu.SemaphoreType.DMA((24,)),
        pltpu.SemaphoreType.DMA((10, CHUNKS)),
        pltpu.SemaphoreType.DMA((10, CHUNKS)),
        pltpu.SemaphoreType.DMA((2 * CHUNKS + 1,)),
    ]
    return pl.pallas_call(
        pixel_kernel,
        out_shape=jax.ShapeDtypeStruct((64, 128, 256), BF),
        in_specs=[
            pl.BlockSpec(memory_space=pltpu.SMEM),
            pl.BlockSpec(memory_space=pl.ANY),
            pl.BlockSpec(memory_space=pl.ANY),
        ],
        out_specs=pl.BlockSpec(memory_space=pl.ANY),
        scratch_shapes=scratch,
        compiler_params=pltpu.CompilerParams(
            collective_id=0, has_side_effects=True, vmem_limit_bytes=60 * MIB
        ),
        cost_estimate=pl.CostEstimate(
            flops=6_500_000_000, bytes_accessed=22_000_000, transcendentals=0
        ),
        name="pixel_pass",
    )(coverage.reshape(-1), sketch.reshape(512, 256), gains)


TILES_STEP = 4


def beam_kernel(cov, g, zb, out, acc, split, sems):
    step = pl.program_id(0)

    @pl.when(step == 0)
    def _():
        @pl.loop(0, 128)
        def _(b):
            acc[b] = jnp.zeros((128, 256), F32)

    for tt in range(TILES_STEP):
        rows = zb[tt]
        for s in range(8):
            b = cov[(step * TILES_STEP + tt) * 8 + s]
            acc[b] += lax.dot_general(
                g[tt, s], rows, (((0,), (0,)), ((), ())), preferred_element_type=F32
            )

    @pl.when(step == pl.num_programs(0) - 1)
    def _():
        low = lax.broadcasted_iota(jnp.int32, (16, 8, 256), 1) < 4

        def store(i):
            return pltpu.make_async_copy(
                split.at[:, :, pl.ds(pl.multiple_of(64 * i, 64), 64)],
                out.at[:, :, pl.ds(pl.multiple_of(64 * i, 64), 64)],
                sems.at[i],
            )

        @pl.loop(0, 8)
        def _(i):
            @pl.loop(0, 8)
            def _(j):
                pair = i * 8 + j
                a = acc[2 * pair].reshape(16, 8, 256)
                b = acc[2 * pair + 1].reshape(16, 8, 256)
                at = pl.ds(pl.multiple_of(8 * pair, 8), 8)
                split[:, 0, at, :] = jnp.where(low, a, pltpu.roll(b, 4, 1))
                split[:, 1, at, :] = jnp.where(low, pltpu.roll(a, 4, 1), b)

            store(i).start()

        @pl.loop(0, 8)
        def _(i):
            store(i).wait()


def beam_pass(coverage, gains, rounded):
    spec = pltpu.PrefetchScalarGridSpec(
        num_scalar_prefetch=1,
        grid=(64 // TILES_STEP,),
        in_specs=[
            pl.BlockSpec((TILES_STEP, 8, 128, 128), lambda i, c: (i, 0, 0, 0)),
            pl.BlockSpec((TILES_STEP, 128, 256), lambda i, c: (i, 0, 0)),
        ],
        out_specs=pl.BlockSpec(memory_space=pl.ANY),
        scratch_shapes=[
            pltpu.VMEM((128, 128, 256), F32),
            pltpu.VMEM((16, 2, 512, 256), F32),
            pltpu.SemaphoreType.DMA((8,)),
        ],
    )
    return pl.pallas_call(
        beam_kernel,
        grid_spec=spec,
        out_shape=jax.ShapeDtypeStruct((16, 2, 512, 256), F32),
        compiler_params=pltpu.CompilerParams(vmem_limit_bytes=56 * MIB),
        cost_estimate=pl.CostEstimate(
            flops=4_300_000_000, bytes_accessed=38_000_000, transcendentals=0
        ),
        name="beam_pass",
    )(coverage.reshape(-1), gains, rounded)

SUB = 4
ROWS = 256 // SUB
HALF = ROWS // 2


def sum_kernel(
    part, flat, gram, own, sib, got1, got2, gacc, gout, gsib, gx, gz, gy,
    csend, crecv, rsend, rrecv, gsend, grecv, local,
):
    pix, y, z, x, core = place()
    near = neighbours()
    other = 1 - core

    def rows(h, j):
        return pl.ds(pl.multiple_of(256 * h + ROWS * j, ROWS), ROWS)

    def load(h, j):
        return pltpu.make_async_copy(
            part.at[:, :, core, rows(h, j)], own.at[h, j], local.at[h, j]
        )

    def swap(h, j):
        return pltpu.make_async_remote_copy(
            src_ref=part.at[:, :, other, rows(h, j)], dst_ref=sib.at[h, j],
            send_sem=csend.at[h, j], recv_sem=crecv.at[h, j],
            device_id=near["sib"], device_id_type=MESH,
        )

    for j in range(SUB):
        for h in range(2):
            load(h, j).start()
    greet(("xr", "xl", "zr", "zl", "sib", "yr", "yl", "xo", "zo", "yo"), near)
    for j in range(SUB):
        for h in range(2):
            swap(h, j).start()

    def ring(h, phase):
        if (h == 0) == (phase == 0):
            return x, "xr", "xl"
        return z, "zr", "zl"

    def piece(h, j, phase, d, lo):
        if phase == 0:
            two = pl.ds(0 if lo else 2, 2)
            return own.at[h, j, two, d] if h == 0 else own.at[h, j, d, two]
        n = pl.ds(0 if lo else HALF, HALF)
        return own.at[h, j, d, x, n] if h == 0 else own.at[h, j, z, d, n]

    def msg(h, j, phase, k):
        c, right, left = ring(h, phase)
        got = got1 if phase == 0 else got2
        d, lo, to = (
            (step4(c, 2), True, right),
            (step4(c, 1), False, right),
            (step4(c, 2), False, left),
            (step4(c, 3), True, left),
            (step4(c, 1), True, right),
            (step4(c, 3), False, left),
        )[k]
        return pltpu.make_async_remote_copy(
            src_ref=piece(h, j, phase, d, lo), dst_ref=got.at[h, j, k],
            send_sem=rsend.at[h, j, phase, k], recv_sem=rrecv.at[h, j, phase, k],
            device_id=near[to], device_id_type=MESH,
        )

    def first(h, j, phase):
        for k in range(4):
            msg(h, j, phase, k).start()

    def second(h, j, phase):
        c = ring(h, phase)[0]
        got = got1 if phase == 0 else got2
        msg(h, j, phase, 0).wait_recv()
        mid = piece(h, j, phase, step4(c, 1), True)
        mid[...] += got[h, j, 0]
        msg(h, j, phase, 4).start()
        msg(h, j, phase, 2).wait_recv()
        mid = piece(h, j, phase, step4(c, 3), False)
        mid[...] += got[h, j, 2]
        msg(h, j, phase, 5).start()

    def finish(h, j, phase):
        c = ring(h, phase)[0]
        got = got1 if phase == 0 else got2
        for k in (3, 4, 1, 5):
            msg(h, j, phase, k).wait_recv()
        lo = piece(h, j, phase, c, True)
        lo[...] += got[h, j, 3] + got[h, j, 4]
        hi = piece(h, j, phase, c, False)
        hi[...] += got[h, j, 1] + got[h, j, 5]

    def stage(tau, after, work):
        @pl.when(jnp.logical_and(tau >= after, tau < after + SUB))
        def _():
            for h in range(2):
                work(h, tau - after)

    @pl.loop(0, SUB + 4)
    def _(tau):
        def begin(h, j):
            load(h, j).wait()
            swap(h, j).wait_recv()

            @pl.loop(0, 4)
            def _(i):
                own[h, j, i] += sib[h, j, i]

            first(h, j, 0)

        def turn(h, j):
            finish(h, j, 0)
            first(h, j, 1)

        def end(h, j):
            finish(h, j, 1)
            flat[rows(h, j), :] = own[h, j, z, x]

        stage(tau, 0, begin)
        stage(tau, 1, lambda h, j: second(h, j, 0))
        stage(tau, 2, turn)
        stage(tau, 3, lambda h, j: second(h, j, 1))
        stage(tau, 4, end)

    f = flat[...]
    gacc[...] = lax.dot_general(
        f, f, (((0,), (0,)), ((), ())),
        precision=lax.Precision.HIGHEST, preferred_element_type=F32,
    )

    def gmsg(k, src, dst, to):
        return pltpu.make_async_remote_copy(
            src_ref=src, dst_ref=dst, send_sem=gsend.at[k], recv_sem=grecv.at[k],
            device_id=near[to], device_id_type=MESH,
        )

    def block(at, n, ref=gacc):
        return ref.at[pl.ds(pl.multiple_of(at, n), n)]

    sent = []

    def exchange(k, pairs):
        todo = [gmsg(k + n, *p) for n, p in enumerate(pairs)]
        for m in todo:
            m.start()
        for m in todo:
            m.wait_recv()
        sent.extend(todo)

    base = 128 * core
    exchange(0, [(block(128 * other, 128), gsib, "sib")])
    mine = block(base, 128)
    mine[...] += gsib[...]
    xat = base + 32 * x
    exchange(1, [
        (block(base + 32 * step4(x, d), 32), gx.at[d - 1], to)
        for d, to in ((1, "xr"), (2, "xo"), (3, "xl"))
    ])
    mine = block(xat, 32)
    mine[...] += gx[0] + gx[1] + gx[2]
    zat = xat + 8 * z
    exchange(4, [
        (block(xat + 8 * step4(z, d), 8), gz.at[d - 1], to)
        for d, to in ((1, "zr"), (2, "zo"), (3, "zl"))
    ])
    mine = block(zat, 8)
    gy[y] = mine[...] + (gz[0] + gz[1] + gz[2])
    exchange(7, [(gy.at[y], gy.at[y], to) for to in ("yr", "yo", "yl")])
    mine = block(zat, 8, gout)
    mine[...] = (gy[0] + gy[1]) + (gy[2] + gy[3])
    exchange(10, [(mine, mine, to) for to in ("zr", "zo", "zl")])
    mine = block(xat, 32, gout)
    exchange(13, [(mine, mine, to) for to in ("xr", "xo", "xl")])
    mine = block(base, 128, gout)
    exchange(16, [(mine, mine, "sib")])
    gram[...] = gout[...]
    for m in sent:
        m.wait_send()

    @pl.loop(0, SUB)
    def _(j):
        for h in range(2):
            swap(h, j).wait_send()
            for phase in range(2):
                for k in range(6):
                    msg(h, j, phase, k).wait_send()


def sum_pass(total):
    scratch = [
        pltpu.VMEM((2, SUB, 4, 4, ROWS, 256), F32),
        pltpu.VMEM((2, SUB, 4, 4, ROWS, 256), F32),
        pltpu.VMEM((2, SUB, 6, 2, ROWS, 256), F32),
        pltpu.VMEM((2, SUB, 6, HALF, 256), F32),
        pltpu.VMEM((256, 256), F32),
        pltpu.VMEM((256, 256), F32),
        pltpu.VMEM((128, 256), F32),
        pltpu.VMEM((3, 32, 256), F32),
        pltpu.VMEM((3, 8, 256), F32),
        pltpu.VMEM((4, 8, 256), F32),
        pltpu.SemaphoreType.DMA((2, SUB)),
        pltpu.SemaphoreType.DMA((2, SUB)),
        pltpu.SemaphoreType.DMA((2, SUB, 2, 6)),
        pltpu.SemaphoreType.DMA((2, SUB, 2, 6)),
        pltpu.SemaphoreType.DMA((17,)),
        pltpu.SemaphoreType.DMA((17,)),
        pltpu.SemaphoreType.DMA((2, SUB)),
    ]
    return pl.pallas_call(
        sum_kernel,
        out_shape=(
            jax.ShapeDtypeStruct((512, 256), F32),
            jax.ShapeDtypeStruct((256, 256), F32),
        ),
        in_specs=[pl.BlockSpec(memory_space=pl.ANY)],
        out_specs=(
            pl.BlockSpec(memory_space=pltpu.VMEM),
            pl.BlockSpec(memory_space=pltpu.VMEM),
        ),
        scratch_shapes=scratch,
        compiler_params=pltpu.CompilerParams(
            collective_id=1, has_side_effects=True, vmem_limit_bytes=48 * MIB
        ),
        cost_estimate=pl.CostEstimate(
            flops=500_000_000, bytes_accessed=18_000_000, transcendentals=0
        ),
        name="sum_pass",
    )(total)

PIVOTS = 4


def eliminate(a):
    sub = lax.broadcasted_iota(jnp.int32, (8, 128), 0)
    lane = lax.broadcasted_iota(jnp.int32, (8, 128), 1)
    rows = [a[8 * i : 8 * i + 8] for i in range(16)]
    inv = [(lane == sub + 8 * i).astype(F32) for i in range(16)]
    for start in range(0, 128, PIVOTS):
        g = start // 8
        cols = [
            [jnp.broadcast_to(r[:, j : j + 1], (8, 128)) for r in rows[g:]]
            for j in range(start, start + PIVOTS)
        ]
        for k in range(PIVOTS):
            at = start + k - 8 * g
            one = jnp.broadcast_to(cols[k][0][at : at + 1], (8, 128))
            scale = 1.0 / one
            head = jnp.broadcast_to(rows[g][at : at + 1], (8, 128))
            head_inv = jnp.broadcast_to(inv[g][at : at + 1], (8, 128))
            heads = [
                jnp.broadcast_to(cols[m][0][at : at + 1], (8, 128))
                for m in range(k + 1, PIVOTS)
            ]
            for i in range(g, 16):
                f = cols[k][i - g] * scale
                if i == g:
                    f = jnp.where(sub > at, f, 0.0)
                for n, m in enumerate(range(k + 1, PIVOTS)):
                    cols[m][i - g] = cols[m][i - g] - f * heads[n]
                rows[i] = rows[i] - f * head
                inv[i] = inv[i] - f * head_inv
    u = jnp.concatenate(rows, axis=0)
    w = jnp.concatenate(inv, axis=0)
    return u, w


def mm(a, b, ca=1, cb=0):
    return lax.dot_general(
        a, b, (((ca,), (cb,)), ((), ())),
        precision=lax.Precision.HIGHEST, preferred_element_type=F32,
    )


def factor_half(a):
    u, w = eliminate(a)
    r = lax.broadcasted_iota(jnp.int32, (128, 128), 0)
    c = lax.broadcasted_iota(jnp.int32, (128, 128), 1)
    d = jnp.sum(jnp.where(r == c, u, 0.0), axis=1, keepdims=True)
    root = 1.0 / jnp.sqrt(d)
    return jnp.where(c >= r, u, 0.0) * root, w * root


def finish_kernel(gram, flat, basis, factor):
    unit = 1.0 / BEAMS**0.5
    r11, m11 = factor_half(gram[:128, :128])
    factor[:128, :128] = r11 * unit
    r12 = mm(m11, gram[:128, 128:])
    factor[:128, 128:] = r12 * unit
    factor[128:, :128] = jnp.zeros((128, 128), F32)
    r22, m22 = factor_half(gram[128:, 128:] - mm(r12, r12, 0, 0))
    factor[128:, 128:] = r22 * unit
    up = BEAMS**0.5
    left = mm(flat[:, :128], m11, 1, 1)
    basis[:, :128] = left * up
    basis[:, 128:] = mm(flat[:, 128:] - mm(left, r12), m22 * up, 1, 1)


def finish(gram, flat):
    vmem = pl.BlockSpec(memory_space=pltpu.VMEM)
    return pl.pallas_call(
        finish_kernel,
        out_shape=(
            jax.ShapeDtypeStruct((512, 256), F32),
            jax.ShapeDtypeStruct((256, 256), F32),
        ),
        in_specs=[vmem, vmem],
        out_specs=(vmem, vmem),
        compiler_params=pltpu.CompilerParams(vmem_limit_bytes=24 * MIB),
        name="finish",
    )(gram, flat)


def local(sketch, gains, coverage):
    rounded = pixel_pass(sketch, gains, coverage)
    total = beam_pass(coverage, gains, rounded)
    flat, gram = sum_pass(total.reshape(4, 4, 2, 512, 256))
    basis, factor = finish(gram, flat)
    return basis.reshape(sketch.shape), factor


def solution(mesh):
    return jax.shard_map(
        local,
        mesh=mesh,
        in_specs=(P("beam", "pix", None), P("pix", "beam", None, None), P("pix", "beam")),
        out_specs=(P("beam", "pix", None), P()),
        check_vma=False,
    )
```

```python
import functools

import jax
import jax.numpy as jnp
from jax import lax
from jax.experimental import pallas as pl
from jax.experimental.pallas import tpu as pltpu
from jax.sharding import PartitionSpec as P

BEAMS = 65536
BF = jnp.bfloat16
F32 = jnp.float32
MESH = pl.DeviceIdType.MESH
MIB = 1 << 20


PLANE = [(n // 4, n % 4) for n in range(1, 16)]


def place():
    pix = lax.axis_index("pix")
    y = lax.axis_index("beam")
    core = lax.rem(pix, 2)
    x = lax.rem(lax.div(pix, 2), 4)
    z = lax.div(pix, 8)
    return pix, y, z, x, core


def step4(v, d):
    return lax.rem(v + d, 4)


def neighbours():
    pix, y, z, x, core = place()

    def at(zz, xx, cc):
        return ((zz * 4 + xx) * 2 + cc, y)

    return dict(
        xr=at(z, step4(x, 1), core),
        xl=at(z, step4(x, 3), core),
        zr=at(step4(z, 1), x, core),
        zl=at(step4(z, 3), x, core),
        sib=at(z, x, 1 - core),
        yr=(pix, step4(y, 1)),
        yl=(pix, step4(y, 3)),
        yo=(pix, step4(y, 2)),
        **{
            "p%d" % n: at(step4(z, dz), step4(x, dx), core)
            for n, (dz, dx) in enumerate(PLANE)
        },
    )


def greet(names, near):
    barrier = pltpu.get_barrier_semaphore()
    for name in names:
        pl.semaphore_signal(barrier, inc=1, device_id=near[name], device_id_type=MESH)
    pl.semaphore_wait(barrier, len(names))


CHUNKS = 8


def pixel_kernel(
    cov, sk, gains, out, raw, om, gbuf, zf, zs, zb, got, csend,
    gsend, grecv, bsend, brecv, local,
):
    pix, y, z, x, core = place()
    near = neighbours()

    def load(i):
        return pltpu.make_async_copy(
            gains.at[pl.ds(8 * i, 8)], gbuf.at[pl.ds(8 * i, 8)], local.at[i]
        )

    mine = pltpu.make_async_copy(sk, raw.at[z, x, core], local.at[CHUNKS])
    mine.start()
    greet(("xr", "xl", "zr", "zl", "sib", "yr", "yl"), near)
    mine.wait()

    def send(k, ref, to):
        return pltpu.make_async_remote_copy(
            src_ref=ref, dst_ref=ref, send_sem=gsend.at[k], recv_sem=grecv.at[k],
            device_id=near[to], device_id_type=MESH,
        )

    lo, hi = pl.ds(0, 256), pl.ds(256, 256)
    a1 = raw.at[z, x, core, lo]
    b1 = raw.at[z, x, core, hi]
    cp = {}

    def go(k, ref, to):
        cp[k] = send(k, ref, to)
        cp[k].start()

    go(0, a1, "xr")
    go(1, a1, "xl")
    go(2, b1, "zr")
    go(3, b1, "zl")
    for i in range(CHUNKS):
        load(i).start()
    xm, xp, xo = step4(x, 3), step4(x, 1), step4(x, 2)
    zm, zp, zo = step4(z, 3), step4(z, 1), step4(z, 2)
    cp[0].wait_recv()
    go(4, raw.at[z, xm, core, pl.ds(0, 128)], "xr")
    cp[1].wait_recv()
    go(5, raw.at[z, xp, core, pl.ds(128, 128)], "xl")
    cp[2].wait_recv()
    go(6, raw.at[zm, x, core, pl.ds(256, 128)], "zr")
    cp[3].wait_recv()
    go(7, raw.at[zp, x, core, pl.ds(384, 128)], "zl")
    cp[4].wait_recv()
    cp[5].wait_recv()
    row = raw.at[z, :, core, lo]
    go(8, row, "zr")
    go(9, row, "zl")
    cp[6].wait_recv()
    cp[7].wait_recv()
    col = raw.at[:, x, core, hi]
    go(10, col, "xr")
    go(11, col, "xl")
    go(12, row, "sib")
    go(13, col, "sib")
    cp[8].wait_recv()
    go(14, raw.at[zm, pl.ds(0, 2), core, lo], "zr")
    cp[9].wait_recv()
    go(15, raw.at[zp, pl.ds(2, 2), core, lo], "zl")
    cp[10].wait_recv()
    go(16, raw.at[pl.ds(0, 2), xm, core, hi], "xr")
    cp[11].wait_recv()
    go(17, raw.at[pl.ds(2, 2), xp, core, hi], "xl")
    go(18, raw.at[zm, :, core, lo], "sib")
    go(19, raw.at[zp, :, core, lo], "sib")
    go(20, raw.at[:, xm, core, hi], "sib")
    go(21, raw.at[:, xp, core, hi], "sib")
    cp[14].wait_recv()
    cp[15].wait_recv()
    go(22, raw.at[zo, :, core, lo], "sib")
    cp[16].wait_recv()
    cp[17].wait_recv()
    go(23, raw.at[:, xo, core, hi], "sib")
    for k in (12, 13, 18, 19, 20, 21, 22, 23):
        cp[k].wait_recv()

    o = lax.broadcasted_iota(jnp.int32, (256, 256), 0)
    c = lax.broadcasted_iota(jnp.int32, (256, 256), 1)
    from_row = ((o % 64) // 4) * 16 + (o // 64) * 4 + o % 4
    swap = (c == from_row).astype(F32).astype(BF)

    @pl.loop(0, 32, unroll=4)
    def _(q):
        for g in range(2):
            part = raw[pl.ds(2 * g, 2), :, :, pl.ds(pl.multiple_of(16 * q, 16), 16), :]
            part = part.reshape(256, 256)
            turned = jnp.dot(swap, part, preferred_element_type=F32).astype(BF)
            om[pl.ds(4 * q, 4), pl.ds(64 * g, 64), :] = turned.reshape(4, 64, 256)

    c0, c1, c2, c3 = y, step4(y, 1), step4(y, 2), step4(y, 3)

    def rc(k, i, src, dst, to):
        return pltpu.make_async_remote_copy(
            src_ref=src, dst_ref=dst, send_sem=bsend.at[k, i], recv_sem=brecv.at[k, i],
            device_id=near[to], device_id_type=MESH,
        )

    def copies(i):
        t = 8 * i
        own = zb.at[pl.ds(t + 2 * c0, 2)]
        left = zb.at[t + 2 * c3]
        right = zb.at[t + 2 * c1 + 1]
        table = (
            (zs.at[t + 2 * c2], got.at[0, i], "yr"),
            (zs.at[t + 2 * c1 + 1], got.at[1, i], "yr"),
            (zs.at[t + 2 * c2 + 1], got.at[2, i], "yl"),
            (zs.at[t + 2 * c3], got.at[3, i], "yl"),
            (csend.at[0, i], got.at[4, i], "yr"),
            (csend.at[1, i], got.at[5, i], "yl"),
            (own, own, "yr"),
            (own, own, "yl"),
            (left, left, "yr"),
            (right, right, "yl"),
        )
        return lambda k: rc(k, i, *table[k])

    def store(i):
        return pltpu.make_async_copy(
            zb.at[pl.ds(8 * i, 8)], out.at[pl.ds(8 * i, 8)], local.at[CHUNKS + 1 + i]
        )

    @pl.loop(0, CHUNKS + 4)
    def _(tau):
        @pl.when(tau < CHUNKS)
        def _():
            load(tau).wait()

            @pl.loop(0, 8, unroll=4)
            def _(tt):
                t = tau * 8 + tt
                lhs = jnp.concatenate([gbuf[t, s] for s in range(8)], axis=1)
                rhs = jnp.concatenate([om[cov[t * 8 + s]] for s in range(8)], axis=0)
                acc = jnp.dot(lhs, rhs, preferred_element_type=F32)
                zf[t] = acc
                zs[t] = acc.astype(BF)

            m = copies(tau)
            for k in range(4):
                m(k).start()

        @pl.when(jnp.logical_and(tau >= 1, tau < CHUNKS + 1))
        def _():
            i = tau - 1
            m = copies(i)
            m(0).wait_recv()
            csend[0, i] = (got[0, i].astype(F32) + zf[8 * i + 2 * c1]).astype(BF)
            m(4).start()
            m(2).wait_recv()
            csend[1, i] = (got[2, i].astype(F32) + zf[8 * i + 2 * c3 + 1]).astype(BF)
            m(5).start()

        @pl.when(jnp.logical_and(tau >= 2, tau < CHUNKS + 2))
        def _():
            i = tau - 2
            m = copies(i)
            m(3).wait_recv()
            m(4).wait_recv()
            t = 8 * i + 2 * c0
            zb[t] = (zf[t] + got[3, i].astype(F32) + got[4, i].astype(F32)).astype(BF)
            m(1).wait_recv()
            m(5).wait_recv()
            zb[t + 1] = (zf[t + 1] + got[1, i].astype(F32) + got[5, i].astype(F32)).astype(BF)
            m(6).start()
            m(7).start()

        @pl.when(jnp.logical_and(tau >= 3, tau < CHUNKS + 3))
        def _():
            m = copies(tau - 3)
            m(6).wait_recv()
            m(8).start()
            m(7).wait_recv()
            m(9).start()

        @pl.when(tau >= 4)
        def _():
            m = copies(tau - 4)
            m(8).wait_recv()
            m(9).wait_recv()
            store(tau - 4).start()

    for k in range(24):
        cp[k].wait_send()

    @pl.loop(0, CHUNKS)
    def _(i):
        m = copies(i)
        for k in range(10):
            m(k).wait_send()
        store(i).wait()


def pixel_pass(sketch, gains, coverage):
    scratch = [
        pltpu.VMEM((4, 4, 2, 512, 256), BF),
        pltpu.VMEM((128, 128, 256), BF),
        pltpu.VMEM((64, 8, 128, 128), BF),
        pltpu.VMEM((64, 128, 256), F32),
        pltpu.VMEM((64, 128, 256), BF),
        pltpu.VMEM((64, 128, 256), BF),
        pltpu.VMEM((6, CHUNKS, 128, 256), BF),
        pltpu.VMEM((2, CHUNKS, 128, 256), BF),
        pltpu.SemaphoreType.DMA((24,)),
        pltpu.SemaphoreType.DMA((24,)),
        pltpu.SemaphoreType.DMA((10, CHUNKS)),
        pltpu.SemaphoreType.DMA((10, CHUNKS)),
        pltpu.SemaphoreType.DMA((2 * CHUNKS + 1,)),
    ]
    return pl.pallas_call(
        pixel_kernel,
        out_shape=jax.ShapeDtypeStruct((64, 128, 256), BF),
        in_specs=[
            pl.BlockSpec(memory_space=pltpu.SMEM),
            pl.BlockSpec(memory_space=pl.ANY),
            pl.BlockSpec(memory_space=pl.ANY),
        ],
        out_specs=pl.BlockSpec(memory_space=pl.ANY),
        scratch_shapes=scratch,
        compiler_params=pltpu.CompilerParams(
            collective_id=0, has_side_effects=True, vmem_limit_bytes=60 * MIB
        ),
        cost_estimate=pl.CostEstimate(
            flops=6_500_000_000, bytes_accessed=22_000_000, transcendentals=0
        ),
        name="pixel_pass",
    )(coverage.reshape(-1), sketch.reshape(512, 256), gains)


TILES_STEP = 16


def beam_kernel(cov, g, zb, out, acc, split, sems):
    step = pl.program_id(0)

    @pl.when(step == 0)
    def _():
        @pl.loop(0, 128)
        def _(b):
            acc[b] = jnp.zeros((128, 256), F32)

    @pl.loop(0, TILES_STEP, unroll=4)
    def _(tt):
        rows = zb[tt]
        for s in range(8):
            b = cov[(step * TILES_STEP + tt) * 8 + s]
            acc[b] += lax.dot_general(
                g[tt, s], rows, (((0,), (0,)), ((), ())), preferred_element_type=F32
            )

    @pl.when(step == pl.num_programs(0) - 1)
    def _():
        low = lax.broadcasted_iota(jnp.int32, (16, 8, 256), 1) < 4

        def store(i):
            return pltpu.make_async_copy(
                split.at[:, :, pl.ds(pl.multiple_of(64 * i, 64), 64)],
                out.at[:, :, pl.ds(pl.multiple_of(64 * i, 64), 64)],
                sems.at[i],
            )

        @pl.loop(0, 8)
        def _(i):
            @pl.loop(0, 8)
            def _(j):
                pair = i * 8 + j
                a = acc[2 * pair].reshape(16, 8, 256)
                b = acc[2 * pair + 1].reshape(16, 8, 256)
                at = pl.ds(pl.multiple_of(8 * pair, 8), 8)
                split[:, 0, at, :] = jnp.where(low, a, pltpu.roll(b, 4, 1))
                split[:, 1, at, :] = jnp.where(low, pltpu.roll(a, 4, 1), b)

            store(i).start()

        @pl.loop(0, 8)
        def _(i):
            store(i).wait()


def beam_pass(coverage, gains, rounded):
    spec = pltpu.PrefetchScalarGridSpec(
        num_scalar_prefetch=1,
        grid=(64 // TILES_STEP,),
        in_specs=[
            pl.BlockSpec((TILES_STEP, 8, 128, 128), lambda i, c: (i, 0, 0, 0)),
            pl.BlockSpec((TILES_STEP, 128, 256), lambda i, c: (i, 0, 0)),
        ],
        out_specs=pl.BlockSpec(memory_space=pl.ANY),
        scratch_shapes=[
            pltpu.VMEM((128, 128, 256), F32),
            pltpu.VMEM((16, 2, 512, 256), F32),
            pltpu.SemaphoreType.DMA((8,)),
        ],
    )
    return pl.pallas_call(
        beam_kernel,
        grid_spec=spec,
        out_shape=jax.ShapeDtypeStruct((16, 2, 512, 256), F32),
        compiler_params=pltpu.CompilerParams(vmem_limit_bytes=56 * MIB),
        cost_estimate=pl.CostEstimate(
            flops=4_300_000_000, bytes_accessed=38_000_000, transcendentals=0
        ),
        name="beam_pass",
    )(coverage.reshape(-1), gains, rounded)

SUB = 4
ROWS = 256 // SUB
HALF = ROWS // 2


def sum_kernel(
    part, flat, gram, own, sib, got1, got2, gacc, gout, gsib, gz, gy,
    csend, crecv, rsend, rrecv, gsend, grecv, local,
):
    pix, y, z, x, core = place()
    near = neighbours()
    other = 1 - core

    def rows(h, j):
        return pl.ds(pl.multiple_of(256 * h + ROWS * j, ROWS), ROWS)

    def load(h, j):
        return pltpu.make_async_copy(
            part.at[:, :, core, rows(h, j)], own.at[h, j], local.at[h, j]
        )

    def swap(h, j):
        return pltpu.make_async_remote_copy(
            src_ref=part.at[:, :, other, rows(h, j)], dst_ref=sib.at[h, j],
            send_sem=csend.at[h, j], recv_sem=crecv.at[h, j],
            device_id=near["sib"], device_id_type=MESH,
        )

    for j in range(SUB):
        for h in range(2):
            load(h, j).start()
    plane = tuple("p%d" % n for n in range(15))
    greet(plane + ("sib", "yr", "yl", "yo"), near)
    for j in range(SUB):
        for h in range(2):
            swap(h, j).start()

    def ring(h, phase):
        if (h == 0) == (phase == 0):
            return x, "xr", "xl"
        return z, "zr", "zl"

    def piece(h, j, phase, d, lo):
        if phase == 0:
            two = pl.ds(0 if lo else 2, 2)
            return own.at[h, j, two, d] if h == 0 else own.at[h, j, d, two]
        n = pl.ds(0 if lo else HALF, HALF)
        return own.at[h, j, d, x, n] if h == 0 else own.at[h, j, z, d, n]

    def msg(h, j, phase, k):
        c, right, left = ring(h, phase)
        got = got1 if phase == 0 else got2
        d, lo, to = (
            (step4(c, 2), True, right),
            (step4(c, 1), False, right),
            (step4(c, 2), False, left),
            (step4(c, 3), True, left),
            (step4(c, 1), True, right),
            (step4(c, 3), False, left),
        )[k]
        return pltpu.make_async_remote_copy(
            src_ref=piece(h, j, phase, d, lo), dst_ref=got.at[h, j, k],
            send_sem=rsend.at[h, j, phase, k], recv_sem=rrecv.at[h, j, phase, k],
            device_id=near[to], device_id_type=MESH,
        )

    def first(h, j, phase):
        for k in range(4):
            msg(h, j, phase, k).start()

    def second(h, j, phase):
        c = ring(h, phase)[0]
        got = got1 if phase == 0 else got2
        msg(h, j, phase, 0).wait_recv()
        mid = piece(h, j, phase, step4(c, 1), True)
        mid[...] += got[h, j, 0]
        msg(h, j, phase, 4).start()
        msg(h, j, phase, 2).wait_recv()
        mid = piece(h, j, phase, step4(c, 3), False)
        mid[...] += got[h, j, 2]
        msg(h, j, phase, 5).start()

    def finish(h, j, phase):
        c = ring(h, phase)[0]
        got = got1 if phase == 0 else got2
        for k in (3, 4, 1, 5):
            msg(h, j, phase, k).wait_recv()
        lo = piece(h, j, phase, c, True)
        lo[...] += got[h, j, 3] + got[h, j, 4]
        hi = piece(h, j, phase, c, False)
        hi[...] += got[h, j, 1] + got[h, j, 5]

    def stage(tau, after, work):
        @pl.when(jnp.logical_and(tau >= after, tau < after + SUB))
        def _():
            for h in range(2):
                work(h, tau - after)

    @pl.loop(0, SUB + 4)
    def _(tau):
        def begin(h, j):
            load(h, j).wait()
            swap(h, j).wait_recv()

            @pl.loop(0, 4)
            def _(i):
                own[h, j, i] += sib[h, j, i]

            first(h, j, 0)

        def turn(h, j):
            finish(h, j, 0)
            first(h, j, 1)

        def end(h, j):
            finish(h, j, 1)
            flat[rows(h, j), :] = own[h, j, z, x]

        stage(tau, 0, begin)
        stage(tau, 1, lambda h, j: second(h, j, 0))
        stage(tau, 2, turn)
        stage(tau, 3, lambda h, j: second(h, j, 1))
        stage(tau, 4, end)

    f = flat[...]
    gacc[...] = lax.dot_general(
        f, f, (((0,), (0,)), ((), ())),
        precision=lax.Precision.HIGHEST, preferred_element_type=F32,
    )

    def gmsg(k, src, dst, to):
        return pltpu.make_async_remote_copy(
            src_ref=src, dst_ref=dst, send_sem=gsend.at[k], recv_sem=grecv.at[k],
            device_id=near[to], device_id_type=MESH,
        )

    def block(at, n, ref=gacc):
        return ref.at[pl.ds(pl.multiple_of(at, n), n)]

    sent = []

    def exchange(k, pairs):
        todo = [gmsg(k + n, *p) for n, p in enumerate(pairs)]
        for m in todo:
            m.start()
        for m in todo:
            m.wait_recv()
        sent.extend(todo)

    base = 128 * core
    exchange(0, [(block(128 * other, 128), gsib, "sib")])
    mine = block(base, 128)
    mine[...] += gsib[...]
    def spot(n):
        dz, dx = PLANE[n]
        return base + 8 * (4 * step4(z, dz) + step4(x, dx))

    exchange(1, [
        (block(spot(n), 8), gz.at[n], "p%d" % n) for n in range(15)
    ])
    at = base + 8 * (4 * z + x)
    mine = block(at, 8)
    total = mine[...]
    for n in range(15):
        total = total + gz[n]
    gy[y] = total
    exchange(16, [(gy.at[y], gy.at[y], to) for to in ("yr", "yo", "yl")])
    mine = block(at, 8, gout)
    mine[...] = (gy[0] + gy[1]) + (gy[2] + gy[3])
    exchange(19, [(mine, mine, "p%d" % n) for n in range(15)])
    mine = block(base, 128, gout)
    exchange(34, [(mine, mine, "sib")])
    gram[...] = gout[...]
    for m in sent:
        m.wait_send()

    @pl.loop(0, SUB)
    def _(j):
        for h in range(2):
            swap(h, j).wait_send()
            for phase in range(2):
                for k in range(6):
                    msg(h, j, phase, k).wait_send()


def sum_pass(total):
    scratch = [
        pltpu.VMEM((2, SUB, 4, 4, ROWS, 256), F32),
        pltpu.VMEM((2, SUB, 4, 4, ROWS, 256), F32),
        pltpu.VMEM((2, SUB, 6, 2, ROWS, 256), F32),
        pltpu.VMEM((2, SUB, 6, HALF, 256), F32),
        pltpu.VMEM((256, 256), F32),
        pltpu.VMEM((256, 256), F32),
        pltpu.VMEM((128, 256), F32),
        pltpu.VMEM((15, 8, 256), F32),
        pltpu.VMEM((4, 8, 256), F32),
        pltpu.SemaphoreType.DMA((2, SUB)),
        pltpu.SemaphoreType.DMA((2, SUB)),
        pltpu.SemaphoreType.DMA((2, SUB, 2, 6)),
        pltpu.SemaphoreType.DMA((2, SUB, 2, 6)),
        pltpu.SemaphoreType.DMA((35,)),
        pltpu.SemaphoreType.DMA((35,)),
        pltpu.SemaphoreType.DMA((2, SUB)),
    ]
    return pl.pallas_call(
        sum_kernel,
        out_shape=(
            jax.ShapeDtypeStruct((512, 256), F32),
            jax.ShapeDtypeStruct((256, 256), F32),
        ),
        in_specs=[pl.BlockSpec(memory_space=pl.ANY)],
        out_specs=(
            pl.BlockSpec(memory_space=pltpu.VMEM),
            pl.BlockSpec(memory_space=pltpu.VMEM),
        ),
        scratch_shapes=scratch,
        compiler_params=pltpu.CompilerParams(
            collective_id=1, has_side_effects=True, vmem_limit_bytes=48 * MIB
        ),
        cost_estimate=pl.CostEstimate(
            flops=500_000_000, bytes_accessed=18_000_000, transcendentals=0
        ),
        name="sum_pass",
    )(total)

PIVOTS = 4


def eliminate(a):
    sub = lax.broadcasted_iota(jnp.int32, (8, 128), 0)
    lane = lax.broadcasted_iota(jnp.int32, (8, 128), 1)
    rows = [a[8 * i : 8 * i + 8] for i in range(16)]
    inv = [(lane == sub + 8 * i).astype(F32) for i in range(16)]
    for start in range(0, 128, PIVOTS):
        g = start // 8
        cols = [
            [jnp.broadcast_to(r[:, j : j + 1], (8, 128)) for r in rows[g:]]
            for j in range(start, start + PIVOTS)
        ]
        for k in range(PIVOTS):
            at = start + k - 8 * g
            one = jnp.broadcast_to(cols[k][0][at : at + 1], (8, 128))
            scale = 1.0 / one
            head = jnp.broadcast_to(rows[g][at : at + 1], (8, 128))
            head_inv = jnp.broadcast_to(inv[g][at : at + 1], (8, 128))
            heads = [
                jnp.broadcast_to(cols[m][0][at : at + 1], (8, 128))
                for m in range(k + 1, PIVOTS)
            ]
            for i in range(g, 16):
                f = cols[k][i - g] * scale
                if i == g:
                    f = jnp.where(sub > at, f, 0.0)
                for n, m in enumerate(range(k + 1, PIVOTS)):
                    cols[m][i - g] = cols[m][i - g] - f * heads[n]
                rows[i] = rows[i] - f * head
                inv[i] = inv[i] - f * head_inv
    u = jnp.concatenate(rows, axis=0)
    w = jnp.concatenate(inv, axis=0)
    return u, w


def mm(a, b, ca=1, cb=0):
    return lax.dot_general(
        a, b, (((ca,), (cb,)), ((), ())),
        precision=lax.Precision.HIGHEST, preferred_element_type=F32,
    )


def factor_half(a):
    u, w = eliminate(a)
    r = lax.broadcasted_iota(jnp.int32, (128, 128), 0)
    c = lax.broadcasted_iota(jnp.int32, (128, 128), 1)
    d = jnp.sum(jnp.where(r == c, u, 0.0), axis=1, keepdims=True)
    root = 1.0 / jnp.sqrt(d)
    return jnp.where(c >= r, u, 0.0) * root, w * root


def finish_kernel(gram, flat, basis, factor):
    unit = 1.0 / BEAMS**0.5
    r11, m11 = factor_half(gram[:128, :128])
    factor[:128, :128] = r11 * unit
    r12 = mm(m11, gram[:128, 128:])
    factor[:128, 128:] = r12 * unit
    factor[128:, :128] = jnp.zeros((128, 128), F32)
    r22, m22 = factor_half(gram[128:, 128:] - mm(r12, r12, 0, 0))
    factor[128:, 128:] = r22 * unit
    up = BEAMS**0.5
    left = mm(flat[:, :128], m11, 1, 1)
    basis[:, :128] = left * up
    basis[:, 128:] = mm(flat[:, 128:] - mm(left, r12), m22 * up, 1, 1)


def finish(gram, flat):
    vmem = pl.BlockSpec(memory_space=pltpu.VMEM)
    return pl.pallas_call(
        finish_kernel,
        out_shape=(
            jax.ShapeDtypeStruct((512, 256), F32),
            jax.ShapeDtypeStruct((256, 256), F32),
        ),
        in_specs=[vmem, vmem],
        out_specs=(vmem, vmem),
        compiler_params=pltpu.CompilerParams(vmem_limit_bytes=24 * MIB),
        name="finish",
    )(gram, flat)


def local(sketch, gains, coverage):
    rounded = pixel_pass(sketch, gains, coverage)
    total = beam_pass(coverage, gains, rounded)
    flat, gram = sum_pass(total.reshape(4, 4, 2, 512, 256))
    basis, factor = finish(gram, flat)
    return basis.reshape(sketch.shape), factor


def solution(mesh):
    return jax.shard_map(
        local,
        mesh=mesh,
        in_specs=(P("beam", "pix", None), P("pix", "beam", None, None), P("pix", "beam")),
        out_specs=(P("beam", "pix", None), P()),
        check_vma=False,
    )
```

```python
import functools

import jax
import jax.numpy as jnp
from jax import lax
from jax.experimental import pallas as pl
from jax.experimental.pallas import tpu as pltpu
from jax.sharding import PartitionSpec as P

BEAMS = 65536
BF = jnp.bfloat16
F32 = jnp.float32
MESH = pl.DeviceIdType.MESH
MIB = 1 << 20


PLANE = [(n // 4, n % 4) for n in range(1, 16)]


def place():
    pix = lax.axis_index("pix")
    y = lax.axis_index("beam")
    core = lax.rem(pix, 2)
    x = lax.rem(lax.div(pix, 2), 4)
    z = lax.div(pix, 8)
    return pix, y, z, x, core


def step4(v, d):
    return lax.rem(v + d, 4)


def neighbours():
    pix, y, z, x, core = place()

    def at(zz, xx, cc):
        return ((zz * 4 + xx) * 2 + cc, y)

    return dict(
        xr=at(z, step4(x, 1), core),
        xl=at(z, step4(x, 3), core),
        zr=at(step4(z, 1), x, core),
        zl=at(step4(z, 3), x, core),
        sib=at(z, x, 1 - core),
        yr=(pix, step4(y, 1)),
        yl=(pix, step4(y, 3)),
        yo=(pix, step4(y, 2)),
        **{
            "p%d" % n: at(step4(z, dz), step4(x, dx), core)
            for n, (dz, dx) in enumerate(PLANE)
        },
    )


def greet(names, near):
    barrier = pltpu.get_barrier_semaphore()
    for name in names:
        pl.semaphore_signal(barrier, inc=1, device_id=near[name], device_id_type=MESH)
    pl.semaphore_wait(barrier, len(names))


W = 128
CHUNKS = 4
TC = 64 // CHUNKS
PART = TC // 8


def gatherer(sk, raw, gsend, grecv, local):
    pix, y, z, x, core = place()
    near = neighbours()
    lo, hi = pl.ds(0, 256), pl.ds(256, 256)
    xm, xp, xo = step4(x, 3), step4(x, 1), step4(x, 2)
    zm, zp, zo = step4(z, 3), step4(z, 1), step4(z, 2)
    row = (z, slice(None), core, lo)
    col = (slice(None), x, core, hi)
    table = (
        ((z, x, core, lo), "xr"),
        ((z, x, core, lo), "xl"),
        ((z, x, core, hi), "zr"),
        ((z, x, core, hi), "zl"),
        ((z, xm, core, pl.ds(0, 128)), "xr"),
        ((z, xp, core, pl.ds(128, 128)), "xl"),
        ((zm, x, core, pl.ds(256, 128)), "zr"),
        ((zp, x, core, pl.ds(384, 128)), "zl"),
        (row, "zr"),
        (row, "zl"),
        (col, "xr"),
        (col, "xl"),
        (row, "sib"),
        (col, "sib"),
        ((zm, pl.ds(0, 2), core, lo), "zr"),
        ((zp, pl.ds(2, 2), core, lo), "zl"),
        ((pl.ds(0, 2), xm, core, hi), "xr"),
        ((pl.ds(2, 2), xp, core, hi), "xl"),
        ((zm, slice(None), core, lo), "sib"),
        ((zp, slice(None), core, lo), "sib"),
        ((slice(None), xm, core, hi), "sib"),
        ((slice(None), xp, core, hi), "sib"),
        ((zo, slice(None), core, lo), "sib"),
        ((slice(None), xo, core, hi), "sib"),
    )

    def cp(k):
        at, to = table[k]
        return pltpu.make_async_remote_copy(
            src_ref=raw.at[at], dst_ref=raw.at[at],
            send_sem=gsend.at[k], recv_sem=grecv.at[k],
            device_id=near[to], device_id_type=MESH,
        )

    def load():
        return pltpu.make_async_copy(sk, raw.at[z, x, core], local)

    def pairs(*steps):
        for wait, start in steps:
            for k in wait:
                cp(k).wait_recv()
            for k in start:
                cp(k).start()

    def begin():
        load().wait()
        pairs(((), (0, 1, 2, 3)))

    def relay():
        pairs(((0,), (4,)), ((1,), (5,)), ((2,), (6,)), ((3,), (7,)))

    def second():
        pairs(((4, 5), (8, 9)), ((6, 7), (10, 11, 12, 13)))

    def relay2():
        pairs(
            ((8,), (14,)), ((9,), (15,)), ((10,), (16,)),
            ((11,), (17, 18, 19, 20, 21)),
        )

    def last():
        pairs(((14, 15), (22,)), ((16, 17), (23,)))

    def done():
        pairs(((12, 13, 18, 19, 20, 21, 22, 23), ()))

    def close():
        for k in range(24):
            cp(k).wait_send()

    return load, (begin, relay, second, relay2, last, done), close


def regroup(raw, om):
    o = lax.broadcasted_iota(jnp.int32, (256, 256), 0)
    c = lax.broadcasted_iota(jnp.int32, (256, 256), 1)
    from_row = ((o % 64) // 4) * 16 + (o // 64) * 4 + o % 4
    swap = (c == from_row).astype(F32).astype(BF)

    @pl.loop(0, 32, unroll=4)
    def _(q):
        for g in range(2):
            part = raw[pl.ds(2 * g, 2), :, :, pl.ds(pl.multiple_of(16 * q, 16), 16), :]
            part = part.reshape(256, W)
            turned = jnp.dot(swap, part, preferred_element_type=F32).astype(BF)
            om[pl.ds(4 * q, 4), pl.ds(64 * g, 64), :] = turned.reshape(4, 64, W)


def pixel_sums(cov, om, gains, out, gbuf, zf, zs, zb, got, csend, bsend, brecv, local):
    y = lax.axis_index("beam")
    near = neighbours()
    c0, c1, c2, c3 = y, step4(y, 1), step4(y, 2), step4(y, 3)

    def rc(k, i, src, dst, to):
        return pltpu.make_async_remote_copy(
            src_ref=src, dst_ref=dst, send_sem=bsend.at[k, i], recv_sem=brecv.at[k, i],
            device_id=near[to], device_id_type=MESH,
        )

    def lo(i, c):
        return pl.ds(TC * i + 2 * PART * c, PART)

    def hi(i, c):
        return pl.ds(TC * i + 2 * PART * c + PART, PART)

    def copies(i):
        own = zb.at[pl.ds(TC * i + 2 * PART * c0, 2 * PART)]
        left = zb.at[lo(i, c3)]
        right = zb.at[hi(i, c1)]
        table = (
            (zs.at[lo(i, c2)], got.at[0, i], "yr"),
            (zs.at[hi(i, c1)], got.at[1, i], "yr"),
            (zs.at[hi(i, c2)], got.at[2, i], "yl"),
            (zs.at[lo(i, c3)], got.at[3, i], "yl"),
            (csend.at[0, i], got.at[4, i], "yr"),
            (csend.at[1, i], got.at[5, i], "yl"),
            (own, own, "yr"),
            (own, own, "yl"),
            (left, left, "yr"),
            (right, right, "yl"),
        )
        return lambda k: rc(k, i, *table[k])

    def store(i):
        at = pl.ds(TC * i, TC)
        return pltpu.make_async_copy(zb.at[at], out.at[at], local.at[CHUNKS + i])

    def load(i):
        at = pl.ds(TC * i, TC)
        return pltpu.make_async_copy(gains.at[at], gbuf.at[at], local.at[i])

    def begin(i):
        load(i).wait()

        @pl.loop(0, TC, unroll=4)
        def _(tt):
            t = i * TC + tt
            lhs = jnp.concatenate([gbuf[t, s] for s in range(8)], axis=1)
            rhs = jnp.concatenate([om[cov[t * 8 + s]] for s in range(8)], axis=0)
            acc = jnp.dot(lhs, rhs, preferred_element_type=F32)
            zf[t] = acc
            zs[t] = acc.astype(BF)

        m = copies(i)
        for k in range(4):
            m(k).start()

    def second(i):
        m = copies(i)
        m(0).wait_recv()
        csend[0, i] = (got[0, i].astype(F32) + zf[lo(i, c1)]).astype(BF)
        m(4).start()
        m(2).wait_recv()
        csend[1, i] = (got[2, i].astype(F32) + zf[hi(i, c3)]).astype(BF)
        m(5).start()

    def third(i):
        m = copies(i)
        m(3).wait_recv()
        m(4).wait_recv()
        a = zf[lo(i, c0)] + got[3, i].astype(F32) + got[4, i].astype(F32)
        zb[lo(i, c0)] = a.astype(BF)
        m(1).wait_recv()
        m(5).wait_recv()
        a = zf[hi(i, c0)] + got[1, i].astype(F32) + got[5, i].astype(F32)
        zb[hi(i, c0)] = a.astype(BF)
        m(6).start()
        m(7).start()

    def fourth(i):
        m = copies(i)
        m(6).wait_recv()
        m(8).start()
        m(7).wait_recv()
        m(9).start()

    def fifth(i):
        m = copies(i)
        m(8).wait_recv()
        m(9).wait_recv()
        store(i).start()

    def sixth(i):
        m = copies(i)
        for k in range(10):
            m(k).wait_send()
        store(i).wait()

    def start_loads():
        for i in range(CHUNKS):
            load(i).start()

    return start_loads, (begin, second, third, fourth, fifth, sixth)


def run_stages(tau, stages, count, after=0):
    for n, work in enumerate(stages):

        @pl.when(jnp.logical_and(tau >= after + n, tau < after + n + count))
        def _():
            work(tau - after - n)


PIXEL_SCRATCH = [
    pltpu.VMEM((64, 8, 128, 128), BF),
    pltpu.VMEM((64, 128, W), F32),
    pltpu.VMEM((64, 128, W), BF),
    pltpu.VMEM((64, 128, W), BF),
    pltpu.VMEM((6, CHUNKS, PART, 128, W), BF),
    pltpu.VMEM((2, CHUNKS, PART, 128, W), BF),
    pltpu.SemaphoreType.DMA((10, CHUNKS)),
    pltpu.SemaphoreType.DMA((10, CHUNKS)),
    pltpu.SemaphoreType.DMA((2 * CHUNKS,)),
]


def first_kernel(cov, sk, gains, out, om_out, raw, om, gsend, grecv, local, *rest):
    near = neighbours()
    parts = [
        gatherer(sk.at[h], raw.at[h], gsend.at[h], grecv.at[h], local.at[h])
        for h in range(2)
    ]
    start_loads, stages = pixel_sums(cov, om.at[0], gains, out, *rest)
    parts[0][0]().start()
    parts[1][0]().start()
    greet(("xr", "xl", "zr", "zl", "sib", "yr", "yl"), near)
    steps = parts[0][1]
    steps[0]()
    start_loads()
    for step in steps[1:]:
        step()
    later = parts[1][1]
    later[0]()
    regroup(raw.at[0], om.at[0])

    def keep():
        return pltpu.make_async_copy(om.at[1], om_out, local.at[2])

    @pl.loop(0, CHUNKS + 5)
    def _(tau):
        run_stages(tau, stages, CHUNKS)
        for step, at in zip(later[1:], GATHER_AT):

            @pl.when(tau == at)
            def _():
                step()

        @pl.when(tau == GATHER_AT[-1])
        def _():
            regroup(raw.at[1], om.at[1])
            keep().start()

    for part in parts:
        part[2]()
    keep().wait()


GATHER_AT = (0, 1, 2, 3, 4)


def first_pass(sketch, gains, coverage):
    scratch = [
        pltpu.VMEM((2, 4, 4, 2, 512, W), BF),
        pltpu.VMEM((2, 128, 128, W), BF),
        pltpu.SemaphoreType.DMA((2, 24)),
        pltpu.SemaphoreType.DMA((2, 24)),
        pltpu.SemaphoreType.DMA((3,)),
        *PIXEL_SCRATCH,
    ]
    hbm = pl.BlockSpec(memory_space=pl.ANY)
    return pl.pallas_call(
        first_kernel,
        out_shape=(
            jax.ShapeDtypeStruct((64, 128, W), BF),
            jax.ShapeDtypeStruct((128, 128, W), BF),
        ),
        in_specs=[pl.BlockSpec(memory_space=pltpu.SMEM), hbm, hbm],
        out_specs=(hbm, hbm),
        scratch_shapes=scratch,
        compiler_params=pltpu.CompilerParams(
            collective_id=0, has_side_effects=True, vmem_limit_bytes=60 * MIB
        ),
        cost_estimate=pl.CostEstimate(
            flops=4_400_000_000, bytes_accessed=24_000_000, transcendentals=0
        ),
        name="first_pass",
    )(coverage.reshape(-1), sketch, gains)


TILES_STEP = 16


def beam_kernel(cov, g, zb, out, acc, split, sems):
    step = pl.program_id(0)

    @pl.when(step == 0)
    def _():
        @pl.loop(0, 128)
        def _(b):
            acc[b] = jnp.zeros((128, W), F32)

    @pl.loop(0, TILES_STEP, unroll=4)
    def _(tt):
        rows = zb[tt]
        for s in range(8):
            b = cov[(step * TILES_STEP + tt) * 8 + s]
            acc[b] += lax.dot_general(
                g[tt, s], rows, (((0,), (0,)), ((), ())), preferred_element_type=F32
            )

    @pl.when(step == pl.num_programs(0) - 1)
    def _():
        low = lax.broadcasted_iota(jnp.int32, (16, 8, W), 1) < 4

        def store(i):
            return pltpu.make_async_copy(
                split.at[:, :, pl.ds(pl.multiple_of(64 * i, 64), 64)],
                out.at[:, :, pl.ds(pl.multiple_of(64 * i, 64), 64)],
                sems.at[i],
            )

        @pl.loop(0, 8)
        def _(i):
            @pl.loop(0, 8)
            def _(j):
                pair = i * 8 + j
                a = acc[2 * pair].reshape(16, 8, W)
                b = acc[2 * pair + 1].reshape(16, 8, W)
                at = pl.ds(pl.multiple_of(8 * pair, 8), 8)
                split[:, 0, at, :] = jnp.where(low, a, pltpu.roll(b, 4, 1))
                split[:, 1, at, :] = jnp.where(low, pltpu.roll(a, 4, 1), b)

            store(i).start()

        @pl.loop(0, 8)
        def _(i):
            store(i).wait()


def beam_pass(coverage, gains, rounded):
    spec = pltpu.PrefetchScalarGridSpec(
        num_scalar_prefetch=1,
        grid=(64 // TILES_STEP,),
        in_specs=[
            pl.BlockSpec((TILES_STEP, 8, 128, 128), lambda i, c: (i, 0, 0, 0)),
            pl.BlockSpec((TILES_STEP, 128, W), lambda i, c: (i, 0, 0)),
        ],
        out_specs=pl.BlockSpec(memory_space=pl.ANY),
        scratch_shapes=[
            pltpu.VMEM((128, 128, W), F32),
            pltpu.VMEM((16, 2, 512, W), F32),
            pltpu.SemaphoreType.DMA((8,)),
        ],
    )
    return pl.pallas_call(
        beam_kernel,
        grid_spec=spec,
        out_shape=jax.ShapeDtypeStruct((16, 2, 512, W), F32),
        compiler_params=pltpu.CompilerParams(vmem_limit_bytes=56 * MIB),
        cost_estimate=pl.CostEstimate(
            flops=4_300_000_000, bytes_accessed=38_000_000, transcendentals=0
        ),
        name="beam_pass",
    )(coverage.reshape(-1), gains, rounded)

SUB = 4
ROWS = 256 // SUB
HALF = ROWS // 2


def row_sums(part, flat, at, own, sib, got1, got2, csend, crecv, rsend, rrecv, local):
    pix, y, z, x, core = place()
    near = neighbours()
    other = 1 - core

    def rows(h, j):
        return pl.ds(pl.multiple_of(256 * h + ROWS * j, ROWS), ROWS)

    def load(h, j):
        return pltpu.make_async_copy(
            part.at[:, :, core, rows(h, j)], own.at[h, j], local.at[h, j]
        )

    def swap(h, j):
        return pltpu.make_async_remote_copy(
            src_ref=part.at[:, :, other, rows(h, j)], dst_ref=sib.at[h, j],
            send_sem=csend.at[h, j], recv_sem=crecv.at[h, j],
            device_id=near["sib"], device_id_type=MESH,
        )

    def start_loads():
        for j in range(SUB):
            for h in range(2):
                load(h, j).start()

    def start_swaps():
        for j in range(SUB):
            for h in range(2):
                swap(h, j).start()

    def ring(h, phase):
        if (h == 0) == (phase == 0):
            return x, "xr", "xl"
        return z, "zr", "zl"

    def piece(h, j, phase, d, lo):
        if phase == 0:
            two = pl.ds(0 if lo else 2, 2)
            return own.at[h, j, two, d] if h == 0 else own.at[h, j, d, two]
        n = pl.ds(0 if lo else HALF, HALF)
        return own.at[h, j, d, x, n] if h == 0 else own.at[h, j, z, d, n]

    def msg(h, j, phase, k):
        c, right, left = ring(h, phase)
        got = got1 if phase == 0 else got2
        d, lo, to = (
            (step4(c, 2), True, right),
            (step4(c, 1), False, right),
            (step4(c, 2), False, left),
            (step4(c, 3), True, left),
            (step4(c, 1), True, right),
            (step4(c, 3), False, left),
        )[k]
        return pltpu.make_async_remote_copy(
            src_ref=piece(h, j, phase, d, lo), dst_ref=got.at[h, j, k],
            send_sem=rsend.at[h, j, phase, k], recv_sem=rrecv.at[h, j, phase, k],
            device_id=near[to], device_id_type=MESH,
        )

    def first(h, j, phase):
        for k in range(4):
            msg(h, j, phase, k).start()

    def second(h, j, phase):
        c = ring(h, phase)[0]
        got = got1 if phase == 0 else got2
        msg(h, j, phase, 0).wait_recv()
        mid = piece(h, j, phase, step4(c, 1), True)
        mid[...] += got[h, j, 0]
        msg(h, j, phase, 4).start()
        msg(h, j, phase, 2).wait_recv()
        mid = piece(h, j, phase, step4(c, 3), False)
        mid[...] += got[h, j, 2]
        msg(h, j, phase, 5).start()

    def finish(h, j, phase):
        c = ring(h, phase)[0]
        got = got1 if phase == 0 else got2
        for k in (3, 4, 1, 5):
            msg(h, j, phase, k).wait_recv()
        lo = piece(h, j, phase, c, True)
        lo[...] += got[h, j, 3] + got[h, j, 4]
        hi = piece(h, j, phase, c, False)
        hi[...] += got[h, j, 1] + got[h, j, 5]

    def both(work):
        def run(j):
            for h in range(2):
                work(h, j)

        return run

    def begin(h, j):
        load(h, j).wait()
        swap(h, j).wait_recv()

        @pl.loop(0, 4)
        def _(i):
            own[h, j, i] += sib[h, j, i]

        first(h, j, 0)

    def turn(h, j):
        finish(h, j, 0)
        first(h, j, 1)

    def end(h, j):
        finish(h, j, 1)
        flat[rows(h, j), at] = own[h, j, z, x]

    def settle(h, j):
        swap(h, j).wait_send()
        for phase in range(2):
            for k in range(6):
                msg(h, j, phase, k).wait_send()

    stages = (
        both(begin),
        both(lambda h, j: second(h, j, 0)),
        both(turn),
        both(lambda h, j: second(h, j, 1)),
        both(end),
        both(settle),
    )

    return start_loads, start_swaps, stages


SUM_SCRATCH = [
    pltpu.VMEM((2, SUB, 4, 4, ROWS, W), F32),
    pltpu.VMEM((2, SUB, 4, 4, ROWS, W), F32),
    pltpu.VMEM((2, SUB, 6, 2, ROWS, W), F32),
    pltpu.VMEM((2, SUB, 6, HALF, W), F32),
    pltpu.SemaphoreType.DMA((2, SUB)),
    pltpu.SemaphoreType.DMA((2, SUB)),
    pltpu.SemaphoreType.DMA((2, SUB, 2, 6)),
    pltpu.SemaphoreType.DMA((2, SUB, 2, 6)),
    pltpu.SemaphoreType.DMA((2, SUB)),
]


def second_kernel(cov, om_in, gains, part, out, flat, om, local, *rest):
    near = neighbours()
    n = len(PIXEL_SCRATCH)
    start_gains, pixel = pixel_sums(cov, om, gains, out, *rest[:n])
    start_own, start_swaps, rows = row_sums(
        part, flat, slice(None), *rest[n:]
    )
    fetch = pltpu.make_async_copy(om_in, om, local)
    fetch.start()
    start_gains()
    start_own()
    greet(("xr", "xl", "zr", "zl", "sib", "yr", "yl"), near)
    start_swaps()
    fetch.wait()

    @pl.loop(0, max(CHUNKS, SUB) + 5)
    def _(tau):
        for n in range(6):
            run_stages(tau, pixel[n : n + 1], CHUNKS, n)
            run_stages(tau, rows[n : n + 1], SUB, n)


def second_pass(coverage, om, gains, part):
    hbm = pl.BlockSpec(memory_space=pl.ANY)
    return pl.pallas_call(
        second_kernel,
        out_shape=(
            jax.ShapeDtypeStruct((64, 128, W), BF),
            jax.ShapeDtypeStruct((512, W), F32),
        ),
        in_specs=[pl.BlockSpec(memory_space=pltpu.SMEM), hbm, hbm, hbm],
        out_specs=(hbm, pl.BlockSpec(memory_space=pltpu.VMEM)),
        scratch_shapes=[
            pltpu.VMEM((128, 128, W), BF),
            pltpu.SemaphoreType.DMA,
            *PIXEL_SCRATCH,
            *SUM_SCRATCH,
        ],
        compiler_params=pltpu.CompilerParams(
            collective_id=1, has_side_effects=True, vmem_limit_bytes=60 * MIB
        ),
        cost_estimate=pl.CostEstimate(
            flops=2_200_000_000, bytes_accessed=32_000_000, transcendentals=0
        ),
        name="second_pass",
    )(coverage.reshape(-1), om, gains, part)


def third_kernel(
    part, flat0, flat, gram, gacc, gout, gsib, gz, gy, gsend, grecv, *rest
):
    pix, y, z, x, core = place()
    near = neighbours()
    other = 1 - core
    start_own, start_swaps, stages = row_sums(part, flat, pl.ds(W, W), *rest)
    start_own()
    plane = tuple("p%d" % n for n in range(15))
    greet(plane + ("sib", "yr", "yl", "yo"), near)
    start_swaps()
    flat[:, :W] = flat0[...]

    @pl.loop(0, SUB + 5)
    def _(tau):
        run_stages(tau, stages, SUB)

    f = flat[...]
    gacc[...] = lax.dot_general(
        f, f, (((0,), (0,)), ((), ())),
        precision=lax.Precision.HIGHEST, preferred_element_type=F32,
    )

    def gmsg(k, src, dst, to):
        return pltpu.make_async_remote_copy(
            src_ref=src, dst_ref=dst, send_sem=gsend.at[k], recv_sem=grecv.at[k],
            device_id=near[to], device_id_type=MESH,
        )

    def block(at, n, ref=gacc):
        return ref.at[pl.ds(pl.multiple_of(at, n), n)]

    sent = []

    def exchange(k, pairs):
        todo = [gmsg(k + n, *p) for n, p in enumerate(pairs)]
        for m in todo:
            m.start()
        for m in todo:
            m.wait_recv()
        sent.extend(todo)

    base = 128 * core
    exchange(0, [(block(128 * other, 128), gsib, "sib")])
    mine = block(base, 128)
    mine[...] += gsib[...]
    def spot(n):
        dz, dx = PLANE[n]
        return base + 8 * (4 * step4(z, dz) + step4(x, dx))

    exchange(1, [
        (block(spot(n), 8), gz.at[n], "p%d" % n) for n in range(15)
    ])
    at = base + 8 * (4 * z + x)
    mine = block(at, 8)
    total = mine[...]
    for n in range(15):
        total = total + gz[n]
    gy[y] = total
    exchange(16, [(gy.at[y], gy.at[y], to) for to in ("yr", "yo", "yl")])
    mine = block(at, 8, gout)
    mine[...] = (gy[0] + gy[1]) + (gy[2] + gy[3])
    exchange(19, [(mine, mine, "p%d" % n) for n in range(15)])
    mine = block(base, 128, gout)
    exchange(34, [(mine, mine, "sib")])
    gram[...] = gout[...]
    for m in sent:
        m.wait_send()


def third_pass(part, flat0):
    vmem = pl.BlockSpec(memory_space=pltpu.VMEM)
    return pl.pallas_call(
        third_kernel,
        out_shape=(
            jax.ShapeDtypeStruct((512, 256), F32),
            jax.ShapeDtypeStruct((256, 256), F32),
        ),
        in_specs=[pl.BlockSpec(memory_space=pl.ANY), vmem],
        out_specs=(vmem, vmem),
        scratch_shapes=[
            pltpu.VMEM((256, 256), F32),
            pltpu.VMEM((256, 256), F32),
            pltpu.VMEM((128, 256), F32),
            pltpu.VMEM((15, 8, 256), F32),
            pltpu.VMEM((4, 8, 256), F32),
            pltpu.SemaphoreType.DMA((35,)),
            pltpu.SemaphoreType.DMA((35,)),
            *SUM_SCRATCH,
        ],
        compiler_params=pltpu.CompilerParams(
            collective_id=2, has_side_effects=True, vmem_limit_bytes=60 * MIB
        ),
        cost_estimate=pl.CostEstimate(
            flops=500_000_000, bytes_accessed=9_000_000, transcendentals=0
        ),
        name="third_pass",
    )(part, flat0)


PIVOTS = 4


def eliminate(a):
    sub = lax.broadcasted_iota(jnp.int32, (8, 128), 0)
    lane = lax.broadcasted_iota(jnp.int32, (8, 128), 1)
    rows = [a[8 * i : 8 * i + 8] for i in range(16)]
    inv = [(lane == sub + 8 * i).astype(F32) for i in range(16)]
    for start in range(0, 128, PIVOTS):
        g = start // 8
        cols = [
            [jnp.broadcast_to(r[:, j : j + 1], (8, 128)) for r in rows[g:]]
            for j in range(start, start + PIVOTS)
        ]
        for k in range(PIVOTS):
            at = start + k - 8 * g
            one = jnp.broadcast_to(cols[k][0][at : at + 1], (8, 128))
            scale = 1.0 / one
            head = jnp.broadcast_to(rows[g][at : at + 1], (8, 128))
            head_inv = jnp.broadcast_to(inv[g][at : at + 1], (8, 128))
            heads = [
                jnp.broadcast_to(cols[m][0][at : at + 1], (8, 128))
                for m in range(k + 1, PIVOTS)
            ]
            for i in range(g, 16):
                f = cols[k][i - g] * scale
                if i == g:
                    f = jnp.where(sub > at, f, 0.0)
                for n, m in enumerate(range(k + 1, PIVOTS)):
                    cols[m][i - g] = cols[m][i - g] - f * heads[n]
                rows[i] = rows[i] - f * head
                inv[i] = inv[i] - f * head_inv
    u = jnp.concatenate(rows, axis=0)
    w = jnp.concatenate(inv, axis=0)
    return u, w


def mm(a, b, ca=1, cb=0):
    return lax.dot_general(
        a, b, (((ca,), (cb,)), ((), ())),
        precision=lax.Precision.HIGHEST, preferred_element_type=F32,
    )


def factor_half(a):
    u, w = eliminate(a)
    r = lax.broadcasted_iota(jnp.int32, (128, 128), 0)
    c = lax.broadcasted_iota(jnp.int32, (128, 128), 1)
    d = jnp.sum(jnp.where(r == c, u, 0.0), axis=1, keepdims=True)
    root = 1.0 / jnp.sqrt(d)
    return jnp.where(c >= r, u, 0.0) * root, w * root


def finish_kernel(gram, flat, basis, factor):
    unit = 1.0 / BEAMS**0.5
    r11, m11 = factor_half(gram[:128, :128])
    factor[:128, :128] = r11 * unit
    r12 = mm(m11, gram[:128, 128:])
    factor[:128, 128:] = r12 * unit
    factor[128:, :128] = jnp.zeros((128, 128), F32)
    r22, m22 = factor_half(gram[128:, 128:] - mm(r12, r12, 0, 0))
    factor[128:, 128:] = r22 * unit
    up = BEAMS**0.5
    left = mm(flat[:, :128], m11, 1, 1)
    basis[:, :128] = left * up
    basis[:, 128:] = mm(flat[:, 128:] - mm(left, r12), m22 * up, 1, 1)


def finish(gram, flat):
    vmem = pl.BlockSpec(memory_space=pltpu.VMEM)
    return pl.pallas_call(
        finish_kernel,
        out_shape=(
            jax.ShapeDtypeStruct((512, 256), F32),
            jax.ShapeDtypeStruct((256, 256), F32),
        ),
        in_specs=[vmem, vmem],
        out_specs=(vmem, vmem),
        compiler_params=pltpu.CompilerParams(vmem_limit_bytes=24 * MIB),
        name="finish",
    )(gram, flat)


def local(sketch, gains, coverage):
    halves = sketch.reshape(512, 2, W).transpose(1, 0, 2)
    shape = (4, 4, 2, 512, W)
    rounded, omega = first_pass(halves, gains, coverage)
    total = beam_pass(coverage, gains, rounded).reshape(shape)
    rounded, flat0 = second_pass(coverage, omega, gains, total)
    total = beam_pass(coverage, gains, rounded).reshape(shape)
    flat, gram = third_pass(total, flat0)
    basis, factor = finish(gram, flat)
    return basis.reshape(sketch.shape), factor


def solution(mesh):
    return jax.shard_map(
        local,
        mesh=mesh,
        in_specs=(P("beam", "pix", None), P("pix", "beam", None, None), P("pix", "beam")),
        out_specs=(P("beam", "pix", None), P()),
        check_vma=False,
    )
```

```python
import functools

import jax
import jax.numpy as jnp
from jax import lax
from jax.experimental import pallas as pl
from jax.experimental.pallas import tpu as pltpu
from jax.sharding import PartitionSpec as P

BEAMS = 65536
BF = jnp.bfloat16
F32 = jnp.float32
MESH = pl.DeviceIdType.MESH
MIB = 1 << 20


PLANE = [(n // 4, n % 4) for n in range(1, 16)]


def place():
    pix = lax.axis_index("pix")
    y = lax.axis_index("beam")
    core = lax.rem(pix, 2)
    x = lax.rem(lax.div(pix, 2), 4)
    z = lax.div(pix, 8)
    return pix, y, z, x, core


def step4(v, d):
    return lax.rem(v + d, 4)


def neighbours():
    pix, y, z, x, core = place()

    def at(zz, xx, cc):
        return ((zz * 4 + xx) * 2 + cc, y)

    return dict(
        xr=at(z, step4(x, 1), core),
        xl=at(z, step4(x, 3), core),
        zr=at(step4(z, 1), x, core),
        zl=at(step4(z, 3), x, core),
        sib=at(z, x, 1 - core),
        yr=(pix, step4(y, 1)),
        yl=(pix, step4(y, 3)),
        yo=(pix, step4(y, 2)),
        **{
            "p%d" % n: at(step4(z, dz), step4(x, dx), core)
            for n, (dz, dx) in enumerate(PLANE)
        },
    )


def greet(names, near):
    barrier = pltpu.get_barrier_semaphore()
    for name in names:
        pl.semaphore_signal(barrier, inc=1, device_id=near[name], device_id_type=MESH)
    pl.semaphore_wait(barrier, len(names))


W = 128
CHUNKS1 = 4
CHUNKS2 = 2


def gatherer(sk, raw, gsend, grecv, local):
    pix, y, z, x, core = place()
    near = neighbours()
    lo, hi = pl.ds(0, 256), pl.ds(256, 256)
    xm, xp, xo = step4(x, 3), step4(x, 1), step4(x, 2)
    zm, zp, zo = step4(z, 3), step4(z, 1), step4(z, 2)
    row = (z, slice(None), core, lo)
    col = (slice(None), x, core, hi)
    table = (
        ((z, x, core, lo), "xr"),
        ((z, x, core, lo), "xl"),
        ((z, x, core, hi), "zr"),
        ((z, x, core, hi), "zl"),
        ((z, xm, core, pl.ds(0, 128)), "xr"),
        ((z, xp, core, pl.ds(128, 128)), "xl"),
        ((zm, x, core, pl.ds(256, 128)), "zr"),
        ((zp, x, core, pl.ds(384, 128)), "zl"),
        (row, "zr"),
        (row, "zl"),
        (col, "xr"),
        (col, "xl"),
        (row, "sib"),
        (col, "sib"),
        ((zm, pl.ds(0, 2), core, lo), "zr"),
        ((zp, pl.ds(2, 2), core, lo), "zl"),
        ((pl.ds(0, 2), xm, core, hi), "xr"),
        ((pl.ds(2, 2), xp, core, hi), "xl"),
        ((zm, slice(None), core, lo), "sib"),
        ((zp, slice(None), core, lo), "sib"),
        ((slice(None), xm, core, hi), "sib"),
        ((slice(None), xp, core, hi), "sib"),
        ((zo, slice(None), core, lo), "sib"),
        ((slice(None), xo, core, hi), "sib"),
    )

    def cp(k):
        at, to = table[k]
        return pltpu.make_async_remote_copy(
            src_ref=raw.at[at], dst_ref=raw.at[at],
            send_sem=gsend.at[k], recv_sem=grecv.at[k],
            device_id=near[to], device_id_type=MESH,
        )

    def load():
        return pltpu.make_async_copy(sk, raw.at[z, x, core], local)

    def pairs(*steps):
        for wait, start in steps:
            for k in wait:
                cp(k).wait_recv()
            for k in start:
                cp(k).start()

    def begin():
        load().wait()
        pairs(((), (0, 1, 2, 3)))

    def relay():
        pairs(((0,), (4,)), ((1,), (5,)), ((2,), (6,)), ((3,), (7,)))

    def second():
        pairs(((4, 5), (8, 9)), ((6, 7), (10, 11, 12, 13)))

    def relay2():
        pairs(
            ((8,), (14,)), ((9,), (15,)), ((10,), (16,)),
            ((11,), (17, 18, 19, 20, 21)),
        )

    def last():
        pairs(((14, 15), (22,)), ((16, 17), (23,)))

    def done():
        pairs(((12, 13, 18, 19, 20, 21, 22, 23), ()))

    def close():
        for k in range(24):
            cp(k).wait_send()

    return load, (begin, relay, second, relay2, last, done), close


def regroup(raw, om):
    o = lax.broadcasted_iota(jnp.int32, (256, 256), 0)
    c = lax.broadcasted_iota(jnp.int32, (256, 256), 1)
    from_row = ((o % 64) // 4) * 16 + (o // 64) * 4 + o % 4
    swap = (c == from_row).astype(F32).astype(BF)

    @pl.loop(0, 32, unroll=4)
    def _(q):
        for g in range(2):
            part = raw[pl.ds(2 * g, 2), :, :, pl.ds(pl.multiple_of(16 * q, 16), 16), :]
            part = part.reshape(256, W)
            turned = jnp.dot(swap, part, preferred_element_type=F32).astype(BF)
            om[pl.ds(4 * q, 4), pl.ds(64 * g, 64), :] = turned.reshape(4, 64, W)


def pixel_sums(chunks, cov, om, gains, out, gbuf, zf, zs, zb, got, csend, bsend, brecv, local):
    tiles = 64 // chunks
    half = tiles // 8
    y = lax.axis_index("beam")
    near = neighbours()
    c0, c1, c2, c3 = y, step4(y, 1), step4(y, 2), step4(y, 3)

    def rc(k, i, src, dst, to):
        return pltpu.make_async_remote_copy(
            src_ref=src, dst_ref=dst, send_sem=bsend.at[k, i], recv_sem=brecv.at[k, i],
            device_id=near[to], device_id_type=MESH,
        )

    def lo(i, c):
        return pl.ds(tiles * i + 2 * half * c, half)

    def hi(i, c):
        return pl.ds(tiles * i + 2 * half * c + half, half)

    def copies(i):
        own = zb.at[pl.ds(tiles * i + 2 * half * c0, 2 * half)]
        left = zb.at[lo(i, c3)]
        right = zb.at[hi(i, c1)]
        table = (
            (zs.at[lo(i, c2)], got.at[0, i], "yr"),
            (zs.at[hi(i, c1)], got.at[1, i], "yr"),
            (zs.at[hi(i, c2)], got.at[2, i], "yl"),
            (zs.at[lo(i, c3)], got.at[3, i], "yl"),
            (csend.at[0, i], got.at[4, i], "yr"),
            (csend.at[1, i], got.at[5, i], "yl"),
            (own, own, "yr"),
            (own, own, "yl"),
            (left, left, "yr"),
            (right, right, "yl"),
        )
        return lambda k: rc(k, i, *table[k])

    def store(i):
        at = pl.ds(tiles * i, tiles)
        return pltpu.make_async_copy(zb.at[at], out.at[at], local.at[chunks + i])

    def load(i):
        at = pl.ds(tiles * i, tiles)
        return pltpu.make_async_copy(gains.at[at], gbuf.at[at], local.at[i])

    def begin(i):
        load(i).wait()

        @pl.loop(0, tiles, unroll=4)
        def _(tt):
            t = i * tiles + tt
            lhs = jnp.concatenate([gbuf[t, s] for s in range(8)], axis=1)
            rhs = jnp.concatenate([om[cov[t * 8 + s]] for s in range(8)], axis=0)
            acc = jnp.dot(lhs, rhs, preferred_element_type=F32)
            zf[t] = acc
            zs[t] = acc.astype(BF)

        m = copies(i)
        for k in range(4):
            m(k).start()

    def second(i):
        m = copies(i)
        m(0).wait_recv()
        csend[0, i] = (got[0, i].astype(F32) + zf[lo(i, c1)]).astype(BF)
        m(4).start()
        m(2).wait_recv()
        csend[1, i] = (got[2, i].astype(F32) + zf[hi(i, c3)]).astype(BF)
        m(5).start()

    def third(i):
        m = copies(i)
        m(3).wait_recv()
        m(4).wait_recv()
        a = zf[lo(i, c0)] + got[3, i].astype(F32) + got[4, i].astype(F32)
        zb[lo(i, c0)] = a.astype(BF)
        m(1).wait_recv()
        m(5).wait_recv()
        a = zf[hi(i, c0)] + got[1, i].astype(F32) + got[5, i].astype(F32)
        zb[hi(i, c0)] = a.astype(BF)
        m(6).start()
        m(7).start()

    def fourth(i):
        m = copies(i)
        m(6).wait_recv()
        m(8).start()
        m(7).wait_recv()
        m(9).start()

    def fifth(i):
        m = copies(i)
        m(8).wait_recv()
        m(9).wait_recv()
        store(i).start()

    def sixth(i):
        m = copies(i)
        for k in range(10):
            m(k).wait_send()
        store(i).wait()

    def start_loads():
        for i in range(chunks):
            load(i).start()

    return start_loads, (begin, second, third, fourth, fifth, sixth)


def run_stages(tau, stages, count, after=0):
    for n, work in enumerate(stages):

        @pl.when(jnp.logical_and(tau >= after + n, tau < after + n + count))
        def _():
            work(tau - after - n)


def pixel_scratch(chunks):
    return [
        pltpu.VMEM((64, 8, 128, 128), BF),
        pltpu.VMEM((64, 128, W), F32),
        pltpu.VMEM((64, 128, W), BF),
        pltpu.VMEM((64, 128, W), BF),
        pltpu.VMEM((6, chunks, 8 // chunks, 128, W), BF),
        pltpu.VMEM((2, chunks, 8 // chunks, 128, W), BF),
        pltpu.SemaphoreType.DMA((10, chunks)),
        pltpu.SemaphoreType.DMA((10, chunks)),
        pltpu.SemaphoreType.DMA((2 * chunks,)),
    ]


def first_kernel(cov, sk, gains, out, om_out, raw, om, gsend, grecv, local, *rest):
    near = neighbours()
    parts = [
        gatherer(sk.at[h], raw.at[h], gsend.at[h], grecv.at[h], local.at[h])
        for h in range(2)
    ]
    start_loads, stages = pixel_sums(CHUNKS1, cov, om.at[0], gains, out, *rest)
    parts[0][0]().start()
    parts[1][0]().start()
    greet(("xr", "xl", "zr", "zl", "sib", "yr", "yl"), near)
    steps = parts[0][1]
    steps[0]()
    start_loads()
    for step in steps[1:]:
        step()
    later = parts[1][1]
    later[0]()
    regroup(raw.at[0], om.at[0])

    def keep():
        return pltpu.make_async_copy(om.at[1], om_out, local.at[2])

    @pl.loop(0, CHUNKS1 + 5)
    def _(tau):
        run_stages(tau, stages, CHUNKS1)
        for step, at in zip(later[1:], GATHER_AT):

            @pl.when(tau == at)
            def _():
                step()

        @pl.when(tau == GATHER_AT[-1])
        def _():
            regroup(raw.at[1], om.at[1])
            keep().start()

    for part in parts:
        part[2]()
    keep().wait()


GATHER_AT = (0, 1, 2, 3, 4)


def first_pass(sketch, gains, coverage):
    scratch = [
        pltpu.VMEM((2, 4, 4, 2, 512, W), BF),
        pltpu.VMEM((2, 128, 128, W), BF),
        pltpu.SemaphoreType.DMA((2, 24)),
        pltpu.SemaphoreType.DMA((2, 24)),
        pltpu.SemaphoreType.DMA((3,)),
        *pixel_scratch(CHUNKS1),
    ]
    hbm = pl.BlockSpec(memory_space=pl.ANY)
    return pl.pallas_call(
        first_kernel,
        out_shape=(
            jax.ShapeDtypeStruct((64, 128, W), BF),
            jax.ShapeDtypeStruct((128, 128, W), BF),
        ),
        in_specs=[pl.BlockSpec(memory_space=pltpu.SMEM), hbm, hbm],
        out_specs=(hbm, hbm),
        scratch_shapes=scratch,
        compiler_params=pltpu.CompilerParams(
            collective_id=0, has_side_effects=True, vmem_limit_bytes=60 * MIB
        ),
        cost_estimate=pl.CostEstimate(
            flops=4_400_000_000, bytes_accessed=24_000_000, transcendentals=0
        ),
        name="first_pass",
    )(coverage.reshape(-1), sketch, gains)


TILES_STEP = 16


def beam_kernel(cov, g, zb, out, acc, split, sems):
    step = pl.program_id(0)

    @pl.when(step == 0)
    def _():
        @pl.loop(0, 128)
        def _(b):
            acc[b] = jnp.zeros((128, W), F32)

    @pl.loop(0, TILES_STEP, unroll=8)
    def _(tt):
        rows = zb[tt]
        for s in range(8):
            b = cov[(step * TILES_STEP + tt) * 8 + s]
            acc[b] += lax.dot_general(
                g[tt, s], rows, (((0,), (0,)), ((), ())), preferred_element_type=F32
            )

    @pl.when(step == pl.num_programs(0) - 1)
    def _():
        low = lax.broadcasted_iota(jnp.int32, (16, 8, W), 1) < 4

        def store(i):
            return pltpu.make_async_copy(
                split.at[:, :, pl.ds(pl.multiple_of(64 * i, 64), 64)],
                out.at[:, :, pl.ds(pl.multiple_of(64 * i, 64), 64)],
                sems.at[i],
            )

        @pl.loop(0, 8)
        def _(i):
            @pl.loop(0, 8)
            def _(j):
                pair = i * 8 + j
                a = acc[2 * pair].reshape(16, 8, W)
                b = acc[2 * pair + 1].reshape(16, 8, W)
                at = pl.ds(pl.multiple_of(8 * pair, 8), 8)
                split[:, 0, at, :] = jnp.where(low, a, pltpu.roll(b, 4, 1))
                split[:, 1, at, :] = jnp.where(low, pltpu.roll(a, 4, 1), b)

            store(i).start()

        @pl.loop(0, 8)
        def _(i):
            store(i).wait()


def beam_pass(coverage, gains, rounded):
    spec = pltpu.PrefetchScalarGridSpec(
        num_scalar_prefetch=1,
        grid=(64 // TILES_STEP,),
        in_specs=[
            pl.BlockSpec((TILES_STEP, 8, 128, 128), lambda i, c: (i, 0, 0, 0)),
            pl.BlockSpec((TILES_STEP, 128, W), lambda i, c: (i, 0, 0)),
        ],
        out_specs=pl.BlockSpec(memory_space=pl.ANY),
        scratch_shapes=[
            pltpu.VMEM((128, 128, W), F32),
            pltpu.VMEM((16, 2, 512, W), F32),
            pltpu.SemaphoreType.DMA((8,)),
        ],
    )
    return pl.pallas_call(
        beam_kernel,
        grid_spec=spec,
        out_shape=jax.ShapeDtypeStruct((16, 2, 512, W), F32),
        compiler_params=pltpu.CompilerParams(vmem_limit_bytes=56 * MIB),
        cost_estimate=pl.CostEstimate(
            flops=4_300_000_000, bytes_accessed=38_000_000, transcendentals=0
        ),
        name="beam_pass",
    )(coverage.reshape(-1), gains, rounded)

SUB = 2
ROWS = 256 // SUB
HALF = ROWS // 2


def row_sums(part, flat, at, own, sib, got1, got2, csend, crecv, rsend, rrecv, local):
    pix, y, z, x, core = place()
    near = neighbours()
    other = 1 - core

    def rows(h, j):
        return pl.ds(pl.multiple_of(256 * h + ROWS * j, ROWS), ROWS)

    def load(h, j):
        return pltpu.make_async_copy(
            part.at[:, :, core, rows(h, j)], own.at[h, j], local.at[h, j]
        )

    def swap(h, j):
        return pltpu.make_async_remote_copy(
            src_ref=part.at[:, :, other, rows(h, j)], dst_ref=sib.at[h, j],
            send_sem=csend.at[h, j], recv_sem=crecv.at[h, j],
            device_id=near["sib"], device_id_type=MESH,
        )

    def start_loads():
        for j in range(SUB):
            for h in range(2):
                load(h, j).start()

    def start_swaps():
        for j in range(SUB):
            for h in range(2):
                swap(h, j).start()

    def ring(h, phase):
        if (h == 0) == (phase == 0):
            return x, "xr", "xl"
        return z, "zr", "zl"

    def piece(h, j, phase, d, lo):
        if phase == 0:
            two = pl.ds(0 if lo else 2, 2)
            return own.at[h, j, two, d] if h == 0 else own.at[h, j, d, two]
        n = pl.ds(0 if lo else HALF, HALF)
        return own.at[h, j, d, x, n] if h == 0 else own.at[h, j, z, d, n]

    def msg(h, j, phase, k):
        c, right, left = ring(h, phase)
        got = got1 if phase == 0 else got2
        d, lo, to = (
            (step4(c, 2), True, right),
            (step4(c, 1), False, right),
            (step4(c, 2), False, left),
            (step4(c, 3), True, left),
            (step4(c, 1), True, right),
            (step4(c, 3), False, left),
        )[k]
        return pltpu.make_async_remote_copy(
            src_ref=piece(h, j, phase, d, lo), dst_ref=got.at[h, j, k],
            send_sem=rsend.at[h, j, phase, k], recv_sem=rrecv.at[h, j, phase, k],
            device_id=near[to], device_id_type=MESH,
        )

    def first(h, j, phase):
        for k in range(4):
            msg(h, j, phase, k).start()

    def second(h, j, phase):
        c = ring(h, phase)[0]
        got = got1 if phase == 0 else got2
        msg(h, j, phase, 0).wait_recv()
        mid = piece(h, j, phase, step4(c, 1), True)
        mid[...] += got[h, j, 0]
        msg(h, j, phase, 4).start()
        msg(h, j, phase, 2).wait_recv()
        mid = piece(h, j, phase, step4(c, 3), False)
        mid[...] += got[h, j, 2]
        msg(h, j, phase, 5).start()

    def finish(h, j, phase):
        c = ring(h, phase)[0]
        got = got1 if phase == 0 else got2
        for k in (3, 4, 1, 5):
            msg(h, j, phase, k).wait_recv()
        lo = piece(h, j, phase, c, True)
        lo[...] += got[h, j, 3] + got[h, j, 4]
        hi = piece(h, j, phase, c, False)
        hi[...] += got[h, j, 1] + got[h, j, 5]

    def both(work):
        def run(j):
            for h in range(2):
                work(h, j)

        return run

    def begin(h, j):
        load(h, j).wait()
        swap(h, j).wait_recv()

        @pl.loop(0, 4)
        def _(i):
            own[h, j, i] += sib[h, j, i]

        first(h, j, 0)

    def turn(h, j):
        finish(h, j, 0)
        first(h, j, 1)

    def end(h, j):
        finish(h, j, 1)
        flat[rows(h, j), at] = own[h, j, z, x]

    def settle(h, j):
        swap(h, j).wait_send()
        for phase in range(2):
            for k in range(6):
                msg(h, j, phase, k).wait_send()

    stages = (
        both(begin),
        both(lambda h, j: second(h, j, 0)),
        both(turn),
        both(lambda h, j: second(h, j, 1)),
        both(end),
        both(settle),
    )

    return start_loads, start_swaps, stages


SUM_SCRATCH = [
    pltpu.VMEM((2, SUB, 4, 4, ROWS, W), F32),
    pltpu.VMEM((2, SUB, 4, 4, ROWS, W), F32),
    pltpu.VMEM((2, SUB, 6, 2, ROWS, W), F32),
    pltpu.VMEM((2, SUB, 6, HALF, W), F32),
    pltpu.SemaphoreType.DMA((2, SUB)),
    pltpu.SemaphoreType.DMA((2, SUB)),
    pltpu.SemaphoreType.DMA((2, SUB, 2, 6)),
    pltpu.SemaphoreType.DMA((2, SUB, 2, 6)),
    pltpu.SemaphoreType.DMA((2, SUB)),
]


def second_kernel(cov, om_in, gains, part, out, flat, om, local, *rest):
    near = neighbours()
    n = len(pixel_scratch(CHUNKS2))
    start_gains, pixel = pixel_sums(CHUNKS2, cov, om, gains, out, *rest[:n])
    start_own, start_swaps, rows = row_sums(
        part, flat, slice(None), *rest[n:]
    )
    fetch = pltpu.make_async_copy(om_in, om, local)
    fetch.start()
    start_gains()
    start_own()
    greet(("xr", "xl", "zr", "zl", "sib", "yr", "yl"), near)
    start_swaps()
    fetch.wait()

    @pl.loop(0, max(CHUNKS2, SUB) + 5)
    def _(tau):
        for n in range(6):
            run_stages(tau, pixel[n : n + 1], CHUNKS2, n)
            run_stages(tau, rows[n : n + 1], SUB, n)


def second_pass(coverage, om, gains, part):
    hbm = pl.BlockSpec(memory_space=pl.ANY)
    return pl.pallas_call(
        second_kernel,
        out_shape=(
            jax.ShapeDtypeStruct((64, 128, W), BF),
            jax.ShapeDtypeStruct((512, W), F32),
        ),
        in_specs=[pl.BlockSpec(memory_space=pltpu.SMEM), hbm, hbm, hbm],
        out_specs=(hbm, pl.BlockSpec(memory_space=pltpu.VMEM)),
        scratch_shapes=[
            pltpu.VMEM((128, 128, W), BF),
            pltpu.SemaphoreType.DMA,
            *pixel_scratch(CHUNKS2),
            *SUM_SCRATCH,
        ],
        compiler_params=pltpu.CompilerParams(
            collective_id=1, has_side_effects=True, vmem_limit_bytes=60 * MIB
        ),
        cost_estimate=pl.CostEstimate(
            flops=2_200_000_000, bytes_accessed=32_000_000, transcendentals=0
        ),
        name="second_pass",
    )(coverage.reshape(-1), om, gains, part)


def third_kernel(
    part, flat0, flat, gram, gacc, gout, gsib, gz, gy, gsend, grecv, *rest
):
    pix, y, z, x, core = place()
    near = neighbours()
    other = 1 - core
    start_own, start_swaps, stages = row_sums(part, flat, pl.ds(W, W), *rest)
    start_own()
    plane = tuple("p%d" % n for n in range(15))
    greet(plane + ("sib", "yr", "yl", "yo"), near)
    start_swaps()
    flat[:, :W] = flat0[...]

    @pl.loop(0, SUB + 5)
    def _(tau):
        run_stages(tau, stages, SUB)

    f = flat[...]
    gacc[...] = lax.dot_general(
        f, f, (((0,), (0,)), ((), ())),
        precision=lax.Precision.HIGHEST, preferred_element_type=F32,
    )

    def gmsg(k, src, dst, to):
        return pltpu.make_async_remote_copy(
            src_ref=src, dst_ref=dst, send_sem=gsend.at[k], recv_sem=grecv.at[k],
            device_id=near[to], device_id_type=MESH,
        )

    def block(at, n, ref=gacc):
        return ref.at[pl.ds(pl.multiple_of(at, n), n)]

    sent = []

    def exchange(k, pairs):
        todo = [gmsg(k + n, *p) for n, p in enumerate(pairs)]
        for m in todo:
            m.start()
        for m in todo:
            m.wait_recv()
        sent.extend(todo)

    base = 128 * core
    exchange(0, [(block(128 * other, 128), gsib, "sib")])
    mine = block(base, 128)
    mine[...] += gsib[...]
    def spot(n):
        dz, dx = PLANE[n]
        return base + 8 * (4 * step4(z, dz) + step4(x, dx))

    exchange(1, [
        (block(spot(n), 8), gz.at[n], "p%d" % n) for n in range(15)
    ])
    at = base + 8 * (4 * z + x)
    mine = block(at, 8)
    total = mine[...]
    for n in range(15):
        total = total + gz[n]
    gy[y] = total
    exchange(16, [(gy.at[y], gy.at[y], to) for to in ("yr", "yo", "yl")])
    mine = block(at, 8, gout)
    mine[...] = (gy[0] + gy[1]) + (gy[2] + gy[3])
    exchange(19, [(mine, mine, "p%d" % n) for n in range(15)])
    mine = block(base, 128, gout)
    exchange(34, [(mine, mine, "sib")])
    gram[...] = gout[...]
    for m in sent:
        m.wait_send()


def third_pass(part, flat0):
    vmem = pl.BlockSpec(memory_space=pltpu.VMEM)
    return pl.pallas_call(
        third_kernel,
        out_shape=(
            jax.ShapeDtypeStruct((512, 256), F32),
            jax.ShapeDtypeStruct((256, 256), F32),
        ),
        in_specs=[pl.BlockSpec(memory_space=pl.ANY), vmem],
        out_specs=(vmem, vmem),
        scratch_shapes=[
            pltpu.VMEM((256, 256), F32),
            pltpu.VMEM((256, 256), F32),
            pltpu.VMEM((128, 256), F32),
            pltpu.VMEM((15, 8, 256), F32),
            pltpu.VMEM((4, 8, 256), F32),
            pltpu.SemaphoreType.DMA((35,)),
            pltpu.SemaphoreType.DMA((35,)),
            *SUM_SCRATCH,
        ],
        compiler_params=pltpu.CompilerParams(
            collective_id=2, has_side_effects=True, vmem_limit_bytes=60 * MIB
        ),
        cost_estimate=pl.CostEstimate(
            flops=500_000_000, bytes_accessed=9_000_000, transcendentals=0
        ),
        name="third_pass",
    )(part, flat0)


PIVOTS = 4


def eliminate(a):
    sub = lax.broadcasted_iota(jnp.int32, (8, 128), 0)
    lane = lax.broadcasted_iota(jnp.int32, (8, 128), 1)
    rows = [a[8 * i : 8 * i + 8] for i in range(16)]
    inv = [(lane == sub + 8 * i).astype(F32) for i in range(16)]
    for start in range(0, 128, PIVOTS):
        g = start // 8
        cols = [
            [jnp.broadcast_to(r[:, j : j + 1], (8, 128)) for r in rows[g:]]
            for j in range(start, start + PIVOTS)
        ]
        for k in range(PIVOTS):
            at = start + k - 8 * g
            one = jnp.broadcast_to(cols[k][0][at : at + 1], (8, 128))
            scale = 1.0 / one
            head = jnp.broadcast_to(rows[g][at : at + 1], (8, 128))
            head_inv = jnp.broadcast_to(inv[g][at : at + 1], (8, 128))
            heads = [
                jnp.broadcast_to(cols[m][0][at : at + 1], (8, 128))
                for m in range(k + 1, PIVOTS)
            ]
            for i in range(g, 16):
                f = cols[k][i - g] * scale
                if i == g:
                    f = jnp.where(sub > at, f, 0.0)
                for n, m in enumerate(range(k + 1, PIVOTS)):
                    cols[m][i - g] = cols[m][i - g] - f * heads[n]
                rows[i] = rows[i] - f * head
                inv[i] = inv[i] - f * head_inv
    u = jnp.concatenate(rows, axis=0)
    w = jnp.concatenate(inv, axis=0)
    return u, w


def mm(a, b, ca=1, cb=0):
    return lax.dot_general(
        a, b, (((ca,), (cb,)), ((), ())),
        precision=lax.Precision.HIGHEST, preferred_element_type=F32,
    )


def factor_half(a):
    u, w = eliminate(a)
    r = lax.broadcasted_iota(jnp.int32, (128, 128), 0)
    c = lax.broadcasted_iota(jnp.int32, (128, 128), 1)
    d = jnp.sum(jnp.where(r == c, u, 0.0), axis=1, keepdims=True)
    root = 1.0 / jnp.sqrt(d)
    return jnp.where(c >= r, u, 0.0) * root, w * root


def finish_kernel(gram, flat, basis, factor):
    unit = 1.0 / BEAMS**0.5
    r11, m11 = factor_half(gram[:128, :128])
    factor[:128, :128] = r11 * unit
    r12 = mm(m11, gram[:128, 128:])
    factor[:128, 128:] = r12 * unit
    factor[128:, :128] = jnp.zeros((128, 128), F32)
    r22, m22 = factor_half(gram[128:, 128:] - mm(r12, r12, 0, 0))
    factor[128:, 128:] = r22 * unit
    up = BEAMS**0.5
    left = mm(flat[:, :128], m11, 1, 1)
    basis[:, :128] = left * up
    basis[:, 128:] = mm(flat[:, 128:] - mm(left, r12), m22 * up, 1, 1)


def finish(gram, flat):
    vmem = pl.BlockSpec(memory_space=pltpu.VMEM)
    return pl.pallas_call(
        finish_kernel,
        out_shape=(
            jax.ShapeDtypeStruct((512, 256), F32),
            jax.ShapeDtypeStruct((256, 256), F32),
        ),
        in_specs=[vmem, vmem],
        out_specs=(vmem, vmem),
        compiler_params=pltpu.CompilerParams(vmem_limit_bytes=24 * MIB),
        name="finish",
    )(gram, flat)


def local(sketch, gains, coverage):
    halves = sketch.reshape(512, 2, W).transpose(1, 0, 2)
    shape = (4, 4, 2, 512, W)
    rounded, omega = first_pass(halves, gains, coverage)
    total = beam_pass(coverage, gains, rounded).reshape(shape)
    rounded, flat0 = second_pass(coverage, omega, gains, total)
    total = beam_pass(coverage, gains, rounded).reshape(shape)
    flat, gram = third_pass(total, flat0)
    basis, factor = finish(gram, flat)
    return basis.reshape(sketch.shape), factor


def solution(mesh):
    return jax.shard_map(
        local,
        mesh=mesh,
        in_specs=(P("beam", "pix", None), P("pix", "beam", None, None), P("pix", "beam")),
        out_specs=(P("beam", "pix", None), P()),
        check_vma=False,
    )
```

```python
import functools

import jax
import jax.numpy as jnp
from jax import lax
from jax.experimental import pallas as pl
from jax.experimental.pallas import tpu as pltpu
from jax.sharding import PartitionSpec as P

BEAMS = 65536
BF = jnp.bfloat16
F32 = jnp.float32
MESH = pl.DeviceIdType.MESH
MIB = 1 << 20


PLANE = [(n // 4, n % 4) for n in range(1, 16)]


def place():
    pix = lax.axis_index("pix")
    y = lax.axis_index("beam")
    core = lax.rem(pix, 2)
    x = lax.rem(lax.div(pix, 2), 4)
    z = lax.div(pix, 8)
    return pix, y, z, x, core


def step4(v, d):
    return lax.rem(v + d, 4)


def neighbours():
    pix, y, z, x, core = place()

    def at(zz, xx, cc):
        return ((zz * 4 + xx) * 2 + cc, y)

    return dict(
        xr=at(z, step4(x, 1), core),
        xl=at(z, step4(x, 3), core),
        zr=at(step4(z, 1), x, core),
        zl=at(step4(z, 3), x, core),
        sib=at(z, x, 1 - core),
        yr=(pix, step4(y, 1)),
        yl=(pix, step4(y, 3)),
        yo=(pix, step4(y, 2)),
        **{
            "p%d" % n: at(step4(z, dz), step4(x, dx), core)
            for n, (dz, dx) in enumerate(PLANE)
        },
    )


def greet(names, near):
    barrier = pltpu.get_barrier_semaphore()
    for name in names:
        pl.semaphore_signal(barrier, inc=1, device_id=near[name], device_id_type=MESH)
    pl.semaphore_wait(barrier, len(names))


W = 128
CHUNKS1 = 4
CHUNKS2 = 2


def gatherer(sk, raw, gsend, grecv, local):
    pix, y, z, x, core = place()
    near = neighbours()
    lo, hi = pl.ds(0, 256), pl.ds(256, 256)
    xm, xp, xo = step4(x, 3), step4(x, 1), step4(x, 2)
    zm, zp, zo = step4(z, 3), step4(z, 1), step4(z, 2)
    row = (z, slice(None), core, lo)
    col = (slice(None), x, core, hi)
    table = (
        ((z, x, core, lo), "xr"),
        ((z, x, core, lo), "xl"),
        ((z, x, core, hi), "zr"),
        ((z, x, core, hi), "zl"),
        ((z, xm, core, pl.ds(0, 128)), "xr"),
        ((z, xp, core, pl.ds(128, 128)), "xl"),
        ((zm, x, core, pl.ds(256, 128)), "zr"),
        ((zp, x, core, pl.ds(384, 128)), "zl"),
        (row, "zr"),
        (row, "zl"),
        (col, "xr"),
        (col, "xl"),
        (row, "sib"),
        (col, "sib"),
        ((zm, pl.ds(0, 2), core, lo), "zr"),
        ((zp, pl.ds(2, 2), core, lo), "zl"),
        ((pl.ds(0, 2), xm, core, hi), "xr"),
        ((pl.ds(2, 2), xp, core, hi), "xl"),
        ((zm, slice(None), core, lo), "sib"),
        ((zp, slice(None), core, lo), "sib"),
        ((slice(None), xm, core, hi), "sib"),
        ((slice(None), xp, core, hi), "sib"),
        ((zo, slice(None), core, lo), "sib"),
        ((slice(None), xo, core, hi), "sib"),
    )

    def cp(k):
        at, to = table[k]
        return pltpu.make_async_remote_copy(
            src_ref=raw.at[at], dst_ref=raw.at[at],
            send_sem=gsend.at[k], recv_sem=grecv.at[k],
            device_id=near[to], device_id_type=MESH,
        )

    def load():
        return pltpu.make_async_copy(sk, raw.at[z, x, core], local)

    def pairs(*steps):
        for wait, start in steps:
            for k in wait:
                cp(k).wait_recv()
            for k in start:
                cp(k).start()

    def begin():
        load().wait()
        pairs(((), (0, 1, 2, 3)))

    def relay():
        pairs(((0,), (4,)), ((1,), (5,)), ((2,), (6,)), ((3,), (7,)))

    def second():
        pairs(((4, 5), (8, 9)), ((6, 7), (10, 11, 12, 13)))

    def relay2():
        pairs(
            ((8,), (14,)), ((9,), (15,)), ((10,), (16,)),
            ((11,), (17, 18, 19, 20, 21)),
        )

    def last():
        pairs(((14, 15), (22,)), ((16, 17), (23,)))

    def done():
        pairs(((12, 13, 18, 19, 20, 21, 22, 23), ()))

    def close():
        for k in range(24):
            cp(k).wait_send()

    return load, (begin, relay, second, relay2, last, done), close


def regroup(raw, om):
    o = lax.broadcasted_iota(jnp.int32, (256, 256), 0)
    c = lax.broadcasted_iota(jnp.int32, (256, 256), 1)
    from_row = ((o % 64) // 4) * 16 + (o // 64) * 4 + o % 4
    swap = (c == from_row).astype(F32).astype(BF)

    @pl.loop(0, 32, unroll=4)
    def _(q):
        for g in range(2):
            part = raw[pl.ds(2 * g, 2), :, :, pl.ds(pl.multiple_of(16 * q, 16), 16), :]
            part = part.reshape(256, W)
            turned = jnp.dot(swap, part, preferred_element_type=F32).astype(BF)
            om[pl.ds(4 * q, 4), pl.ds(64 * g, 64), :] = turned.reshape(4, 64, W)


def pixel_sums(chunks, cov, om, gains, out, gbuf, zf, zs, zb, got, csend, bsend, brecv, local):
    tiles = 64 // chunks
    half = tiles // 8
    y = lax.axis_index("beam")
    near = neighbours()
    c0, c1, c2, c3 = y, step4(y, 1), step4(y, 2), step4(y, 3)

    def rc(k, i, src, dst, to):
        return pltpu.make_async_remote_copy(
            src_ref=src, dst_ref=dst, send_sem=bsend.at[k, i], recv_sem=brecv.at[k, i],
            device_id=near[to], device_id_type=MESH,
        )

    def lo(i, c):
        return pl.ds(tiles * i + 2 * half * c, half)

    def hi(i, c):
        return pl.ds(tiles * i + 2 * half * c + half, half)

    def copies(i):
        own = zb.at[pl.ds(tiles * i + 2 * half * c0, 2 * half)]
        left = zb.at[lo(i, c3)]
        right = zb.at[hi(i, c1)]
        table = (
            (zs.at[lo(i, c2)], got.at[0, i], "yr"),
            (zs.at[hi(i, c1)], got.at[1, i], "yr"),
            (zs.at[hi(i, c2)], got.at[2, i], "yl"),
            (zs.at[lo(i, c3)], got.at[3, i], "yl"),
            (csend.at[0, i], got.at[4, i], "yr"),
            (csend.at[1, i], got.at[5, i], "yl"),
            (own, own, "yr"),
            (own, own, "yl"),
            (left, left, "yr"),
            (right, right, "yl"),
        )
        return lambda k: rc(k, i, *table[k])

    def store(i):
        at = pl.ds(tiles * i, tiles)
        return pltpu.make_async_copy(zb.at[at], out.at[at], local.at[chunks + i])

    def load(i):
        at = pl.ds(tiles * i, tiles)
        return pltpu.make_async_copy(gains.at[at], gbuf.at[at], local.at[i])

    def begin(i):
        load(i).wait()

        @pl.loop(0, tiles, unroll=4)
        def _(tt):
            t = i * tiles + tt
            lhs = jnp.concatenate([gbuf[t, s] for s in range(8)], axis=1)
            rhs = jnp.concatenate([om[cov[t * 8 + s]] for s in range(8)], axis=0)
            acc = jnp.dot(lhs, rhs, preferred_element_type=F32)
            zf[t] = acc
            zs[t] = acc.astype(BF)

        m = copies(i)
        for k in range(4):
            m(k).start()

    def second(i):
        m = copies(i)
        m(0).wait_recv()
        csend[0, i] = (got[0, i].astype(F32) + zf[lo(i, c1)]).astype(BF)
        m(4).start()
        m(2).wait_recv()
        csend[1, i] = (got[2, i].astype(F32) + zf[hi(i, c3)]).astype(BF)
        m(5).start()

    def third(i):
        m = copies(i)
        m(3).wait_recv()
        m(4).wait_recv()
        a = zf[lo(i, c0)] + got[3, i].astype(F32) + got[4, i].astype(F32)
        zb[lo(i, c0)] = a.astype(BF)
        m(1).wait_recv()
        m(5).wait_recv()
        a = zf[hi(i, c0)] + got[1, i].astype(F32) + got[5, i].astype(F32)
        zb[hi(i, c0)] = a.astype(BF)
        m(6).start()
        m(7).start()

    def fourth(i):
        m = copies(i)
        m(6).wait_recv()
        m(8).start()
        m(7).wait_recv()
        m(9).start()

    def fifth(i):
        m = copies(i)
        m(8).wait_recv()
        m(9).wait_recv()
        store(i).start()

    def sixth(i):
        m = copies(i)
        for k in range(10):
            m(k).wait_send()
        store(i).wait()

    def start_loads():
        for i in range(chunks):
            load(i).start()

    return start_loads, (begin, second, third, fourth, fifth, sixth)


def run_stages(tau, stages, count, after=0):
    for n, work in enumerate(stages):

        @pl.when(jnp.logical_and(tau >= after + n, tau < after + n + count))
        def _():
            work(tau - after - n)


def pixel_scratch(chunks):
    return [
        pltpu.VMEM((64, 8, 128, 128), BF),
        pltpu.VMEM((64, 128, W), F32),
        pltpu.VMEM((64, 128, W), BF),
        pltpu.VMEM((64, 128, W), BF),
        pltpu.VMEM((6, chunks, 8 // chunks, 128, W), BF),
        pltpu.VMEM((2, chunks, 8 // chunks, 128, W), BF),
        pltpu.SemaphoreType.DMA((10, chunks)),
        pltpu.SemaphoreType.DMA((10, chunks)),
        pltpu.SemaphoreType.DMA((2 * chunks,)),
    ]


def first_kernel(cov, sk, gains, out, om_out, raw, om, gsend, grecv, local, *rest):
    near = neighbours()
    parts = [
        gatherer(sk.at[h], raw.at[h], gsend.at[h], grecv.at[h], local.at[h])
        for h in range(2)
    ]
    start_loads, stages = pixel_sums(CHUNKS1, cov, om.at[0], gains, out, *rest)
    parts[0][0]().start()
    parts[1][0]().start()
    greet(("xr", "xl", "zr", "zl", "sib", "yr", "yl"), near)
    steps = parts[0][1]
    steps[0]()
    start_loads()
    for step in steps[1:]:
        step()
    later = parts[1][1]
    later[0]()
    regroup(raw.at[0], om.at[0])

    def keep():
        return pltpu.make_async_copy(om.at[1], om_out, local.at[2])

    @pl.loop(0, CHUNKS1 + 5)
    def _(tau):
        run_stages(tau, stages, CHUNKS1)
        for step, at in zip(later[1:], GATHER_AT):

            @pl.when(tau == at)
            def _():
                step()

        @pl.when(tau == GATHER_AT[-1])
        def _():
            regroup(raw.at[1], om.at[1])
            keep().start()

    for part in parts:
        part[2]()
    keep().wait()


GATHER_AT = (0, 1, 2, 3, 4)


def first_pass(sketch, gains, coverage):
    scratch = [
        pltpu.VMEM((2, 4, 4, 2, 512, W), BF),
        pltpu.VMEM((2, 128, 128, W), BF),
        pltpu.SemaphoreType.DMA((2, 24)),
        pltpu.SemaphoreType.DMA((2, 24)),
        pltpu.SemaphoreType.DMA((3,)),
        *pixel_scratch(CHUNKS1),
    ]
    hbm = pl.BlockSpec(memory_space=pl.ANY)
    return pl.pallas_call(
        first_kernel,
        out_shape=(
            jax.ShapeDtypeStruct((64, 128, W), BF),
            jax.ShapeDtypeStruct((128, 128, W), BF),
        ),
        in_specs=[pl.BlockSpec(memory_space=pltpu.SMEM), hbm, hbm],
        out_specs=(hbm, hbm),
        scratch_shapes=scratch,
        compiler_params=pltpu.CompilerParams(
            collective_id=0, has_side_effects=True, vmem_limit_bytes=60 * MIB
        ),
        cost_estimate=pl.CostEstimate(
            flops=4_400_000_000, bytes_accessed=24_000_000, transcendentals=0
        ),
        name="first_pass",
    )(coverage.reshape(-1), sketch, gains)


TILES_STEP = 16


def beam_kernel(cov, g, zb, out, acc, split, sems):
    step = pl.program_id(0)

    @pl.when(step == 0)
    def _():
        @pl.loop(0, 128)
        def _(b):
            acc[b] = jnp.zeros((128, W), F32)

    @pl.loop(0, TILES_STEP, unroll=16)
    def _(tt):
        rows = zb[tt]
        for s in range(8):
            b = cov[(step * TILES_STEP + tt) * 8 + s]
            acc[b] += lax.dot_general(
                g[tt, s], rows, (((0,), (0,)), ((), ())), preferred_element_type=F32
            )

    @pl.when(step == pl.num_programs(0) - 1)
    def _():
        low = lax.broadcasted_iota(jnp.int32, (16, 8, W), 1) < 4

        def store(i):
            return pltpu.make_async_copy(
                split.at[:, :, pl.ds(pl.multiple_of(64 * i, 64), 64)],
                out.at[:, :, pl.ds(pl.multiple_of(64 * i, 64), 64)],
                sems.at[i],
            )

        @pl.loop(0, 8)
        def _(i):
            @pl.loop(0, 8)
            def _(j):
                pair = i * 8 + j
                a = acc[2 * pair].reshape(16, 8, W)
                b = acc[2 * pair + 1].reshape(16, 8, W)
                at = pl.ds(pl.multiple_of(8 * pair, 8), 8)
                split[:, 0, at, :] = jnp.where(low, a, pltpu.roll(b, 4, 1))
                split[:, 1, at, :] = jnp.where(low, pltpu.roll(a, 4, 1), b)

            store(i).start()

        @pl.loop(0, 8)
        def _(i):
            store(i).wait()


def beam_pass(coverage, gains, rounded):
    spec = pltpu.PrefetchScalarGridSpec(
        num_scalar_prefetch=1,
        grid=(64 // TILES_STEP,),
        in_specs=[
            pl.BlockSpec((TILES_STEP, 8, 128, 128), lambda i, c: (i, 0, 0, 0)),
            pl.BlockSpec((TILES_STEP, 128, W), lambda i, c: (i, 0, 0)),
        ],
        out_specs=pl.BlockSpec(memory_space=pl.ANY),
        scratch_shapes=[
            pltpu.VMEM((128, 128, W), F32),
            pltpu.VMEM((16, 2, 512, W), F32),
            pltpu.SemaphoreType.DMA((8,)),
        ],
    )
    return pl.pallas_call(
        beam_kernel,
        grid_spec=spec,
        out_shape=jax.ShapeDtypeStruct((16, 2, 512, W), F32),
        compiler_params=pltpu.CompilerParams(vmem_limit_bytes=56 * MIB),
        cost_estimate=pl.CostEstimate(
            flops=4_300_000_000, bytes_accessed=38_000_000, transcendentals=0
        ),
        name="beam_pass",
    )(coverage.reshape(-1), gains, rounded)

SUB = 2
ROWS = 256 // SUB
HALF = ROWS // 2


def row_sums(part, flat, at, own, sib, got1, got2, csend, crecv, rsend, rrecv, local):
    pix, y, z, x, core = place()
    near = neighbours()
    other = 1 - core

    def rows(h, j):
        return pl.ds(pl.multiple_of(256 * h + ROWS * j, ROWS), ROWS)

    def load(h, j):
        return pltpu.make_async_copy(
            part.at[:, :, core, rows(h, j)], own.at[h, j], local.at[h, j]
        )

    def swap(h, j):
        return pltpu.make_async_remote_copy(
            src_ref=part.at[:, :, other, rows(h, j)], dst_ref=sib.at[h, j],
            send_sem=csend.at[h, j], recv_sem=crecv.at[h, j],
            device_id=near["sib"], device_id_type=MESH,
        )

    def start_loads():
        for j in range(SUB):
            for h in range(2):
                load(h, j).start()

    def start_swaps():
        for j in range(SUB):
            for h in range(2):
                swap(h, j).start()

    def ring(h, phase):
        if (h == 0) == (phase == 0):
            return x, "xr", "xl"
        return z, "zr", "zl"

    def piece(h, j, phase, d, lo):
        if phase == 0:
            two = pl.ds(0 if lo else 2, 2)
            return own.at[h, j, two, d] if h == 0 else own.at[h, j, d, two]
        n = pl.ds(0 if lo else HALF, HALF)
        return own.at[h, j, d, x, n] if h == 0 else own.at[h, j, z, d, n]

    def msg(h, j, phase, k):
        c, right, left = ring(h, phase)
        got = got1 if phase == 0 else got2
        d, lo, to = (
            (step4(c, 2), True, right),
            (step4(c, 1), False, right),
            (step4(c, 2), False, left),
            (step4(c, 3), True, left),
            (step4(c, 1), True, right),
            (step4(c, 3), False, left),
        )[k]
        return pltpu.make_async_remote_copy(
            src_ref=piece(h, j, phase, d, lo), dst_ref=got.at[h, j, k],
            send_sem=rsend.at[h, j, phase, k], recv_sem=rrecv.at[h, j, phase, k],
            device_id=near[to], device_id_type=MESH,
        )

    def first(h, j, phase):
        for k in range(4):
            msg(h, j, phase, k).start()

    def second(h, j, phase):
        c = ring(h, phase)[0]
        got = got1 if phase == 0 else got2
        msg(h, j, phase, 0).wait_recv()
        mid = piece(h, j, phase, step4(c, 1), True)
        mid[...] += got[h, j, 0]
        msg(h, j, phase, 4).start()
        msg(h, j, phase, 2).wait_recv()
        mid = piece(h, j, phase, step4(c, 3), False)
        mid[...] += got[h, j, 2]
        msg(h, j, phase, 5).start()

    def finish(h, j, phase):
        c = ring(h, phase)[0]
        got = got1 if phase == 0 else got2
        for k in (3, 4, 1, 5):
            msg(h, j, phase, k).wait_recv()
        lo = piece(h, j, phase, c, True)
        lo[...] += got[h, j, 3] + got[h, j, 4]
        hi = piece(h, j, phase, c, False)
        hi[...] += got[h, j, 1] + got[h, j, 5]

    def both(work):
        def run(j):
            for h in range(2):
                work(h, j)

        return run

    def begin(h, j):
        load(h, j).wait()
        swap(h, j).wait_recv()

        @pl.loop(0, 4)
        def _(i):
            own[h, j, i] += sib[h, j, i]

        first(h, j, 0)

    def turn(h, j):
        finish(h, j, 0)
        first(h, j, 1)

    def end(h, j):
        finish(h, j, 1)
        flat[rows(h, j), at] = own[h, j, z, x]

    def settle(h, j):
        swap(h, j).wait_send()
        for phase in range(2):
            for k in range(6):
                msg(h, j, phase, k).wait_send()

    stages = (
        both(begin),
        both(lambda h, j: second(h, j, 0)),
        both(turn),
        both(lambda h, j: second(h, j, 1)),
        both(end),
        both(settle),
    )

    return start_loads, start_swaps, stages


SUM_SCRATCH = [
    pltpu.VMEM((2, SUB, 4, 4, ROWS, W), F32),
    pltpu.VMEM((2, SUB, 4, 4, ROWS, W), F32),
    pltpu.VMEM((2, SUB, 6, 2, ROWS, W), F32),
    pltpu.VMEM((2, SUB, 6, HALF, W), F32),
    pltpu.SemaphoreType.DMA((2, SUB)),
    pltpu.SemaphoreType.DMA((2, SUB)),
    pltpu.SemaphoreType.DMA((2, SUB, 2, 6)),
    pltpu.SemaphoreType.DMA((2, SUB, 2, 6)),
    pltpu.SemaphoreType.DMA((2, SUB)),
]


def second_kernel(cov, om_in, gains, part, out, flat, om, local, *rest):
    near = neighbours()
    n = len(pixel_scratch(CHUNKS2))
    start_gains, pixel = pixel_sums(CHUNKS2, cov, om, gains, out, *rest[:n])
    start_own, start_swaps, rows = row_sums(
        part, flat, slice(None), *rest[n:]
    )
    fetch = pltpu.make_async_copy(om_in, om, local)
    fetch.start()
    start_gains()
    start_own()
    greet(("xr", "xl", "zr", "zl", "sib", "yr", "yl"), near)
    start_swaps()
    fetch.wait()

    @pl.loop(0, max(CHUNKS2, SUB) + 5)
    def _(tau):
        for n in range(6):
            run_stages(tau, pixel[n : n + 1], CHUNKS2, n)
            run_stages(tau, rows[n : n + 1], SUB, n)


def second_pass(coverage, om, gains, part):
    hbm = pl.BlockSpec(memory_space=pl.ANY)
    return pl.pallas_call(
        second_kernel,
        out_shape=(
            jax.ShapeDtypeStruct((64, 128, W), BF),
            jax.ShapeDtypeStruct((512, W), F32),
        ),
        in_specs=[pl.BlockSpec(memory_space=pltpu.SMEM), hbm, hbm, hbm],
        out_specs=(hbm, pl.BlockSpec(memory_space=pltpu.VMEM)),
        scratch_shapes=[
            pltpu.VMEM((128, 128, W), BF),
            pltpu.SemaphoreType.DMA,
            *pixel_scratch(CHUNKS2),
            *SUM_SCRATCH,
        ],
        compiler_params=pltpu.CompilerParams(
            collective_id=1, has_side_effects=True, vmem_limit_bytes=60 * MIB
        ),
        cost_estimate=pl.CostEstimate(
            flops=2_200_000_000, bytes_accessed=32_000_000, transcendentals=0
        ),
        name="second_pass",
    )(coverage.reshape(-1), om, gains, part)


def third_kernel(
    part, flat0, flat, gram, gacc, gout, gsib, gz, gy, gsend, grecv, *rest
):
    pix, y, z, x, core = place()
    near = neighbours()
    other = 1 - core
    start_own, start_swaps, stages = row_sums(part, flat, pl.ds(W, W), *rest)
    start_own()
    plane = tuple("p%d" % n for n in range(15))
    greet(plane + ("sib", "yr", "yl", "yo"), near)
    start_swaps()
    flat[:, :W] = flat0[...]

    @pl.loop(0, SUB + 5)
    def _(tau):
        run_stages(tau, stages, SUB)

    f = flat[...]
    gacc[...] = lax.dot_general(
        f, f, (((0,), (0,)), ((), ())),
        precision=lax.Precision.HIGHEST, preferred_element_type=F32,
    )

    def gmsg(k, src, dst, to):
        return pltpu.make_async_remote_copy(
            src_ref=src, dst_ref=dst, send_sem=gsend.at[k], recv_sem=grecv.at[k],
            device_id=near[to], device_id_type=MESH,
        )

    def block(at, n, ref=gacc):
        return ref.at[pl.ds(pl.multiple_of(at, n), n)]

    sent = []

    def exchange(k, pairs):
        todo = [gmsg(k + n, *p) for n, p in enumerate(pairs)]
        for m in todo:
            m.start()
        for m in todo:
            m.wait_recv()
        sent.extend(todo)

    base = 128 * core
    exchange(0, [(block(128 * other, 128), gsib, "sib")])
    mine = block(base, 128)
    mine[...] += gsib[...]
    def spot(n):
        dz, dx = PLANE[n]
        return base + 8 * (4 * step4(z, dz) + step4(x, dx))

    exchange(1, [
        (block(spot(n), 8), gz.at[n], "p%d" % n) for n in range(15)
    ])
    at = base + 8 * (4 * z + x)
    mine = block(at, 8)
    total = mine[...]
    for n in range(15):
        total = total + gz[n]
    gy[y] = total
    exchange(16, [(gy.at[y], gy.at[y], to) for to in ("yr", "yo", "yl")])
    mine = block(at, 8, gout)
    mine[...] = (gy[0] + gy[1]) + (gy[2] + gy[3])
    exchange(19, [(mine, mine, "p%d" % n) for n in range(15)])
    mine = block(base, 128, gout)
    exchange(34, [(mine, mine, "sib")])
    gram[...] = gout[...]
    for m in sent:
        m.wait_send()


def third_pass(part, flat0):
    vmem = pl.BlockSpec(memory_space=pltpu.VMEM)
    return pl.pallas_call(
        third_kernel,
        out_shape=(
            jax.ShapeDtypeStruct((512, 256), F32),
            jax.ShapeDtypeStruct((256, 256), F32),
        ),
        in_specs=[pl.BlockSpec(memory_space=pl.ANY), vmem],
        out_specs=(vmem, vmem),
        scratch_shapes=[
            pltpu.VMEM((256, 256), F32),
            pltpu.VMEM((256, 256), F32),
            pltpu.VMEM((128, 256), F32),
            pltpu.VMEM((15, 8, 256), F32),
            pltpu.VMEM((4, 8, 256), F32),
            pltpu.SemaphoreType.DMA((35,)),
            pltpu.SemaphoreType.DMA((35,)),
            *SUM_SCRATCH,
        ],
        compiler_params=pltpu.CompilerParams(
            collective_id=2, has_side_effects=True, vmem_limit_bytes=60 * MIB
        ),
        cost_estimate=pl.CostEstimate(
            flops=500_000_000, bytes_accessed=9_000_000, transcendentals=0
        ),
        name="third_pass",
    )(part, flat0)


PIVOTS = 4


def eliminate(a):
    sub = lax.broadcasted_iota(jnp.int32, (8, 128), 0)
    lane = lax.broadcasted_iota(jnp.int32, (8, 128), 1)
    rows = [a[8 * i : 8 * i + 8] for i in range(16)]
    inv = [(lane == sub + 8 * i).astype(F32) for i in range(16)]
    for start in range(0, 128, PIVOTS):
        g = start // 8
        cols = [
            [jnp.broadcast_to(r[:, j : j + 1], (8, 128)) for r in rows[g:]]
            for j in range(start, start + PIVOTS)
        ]
        for k in range(PIVOTS):
            at = start + k - 8 * g
            one = jnp.broadcast_to(cols[k][0][at : at + 1], (8, 128))
            scale = 1.0 / one
            head = jnp.broadcast_to(rows[g][at : at + 1], (8, 128))
            head_inv = jnp.broadcast_to(inv[g][at : at + 1], (8, 128))
            heads = [
                jnp.broadcast_to(cols[m][0][at : at + 1], (8, 128))
                for m in range(k + 1, PIVOTS)
            ]
            for i in range(g, 16):
                f = cols[k][i - g] * scale
                if i == g:
                    f = jnp.where(sub > at, f, 0.0)
                for n, m in enumerate(range(k + 1, PIVOTS)):
                    cols[m][i - g] = cols[m][i - g] - f * heads[n]
                rows[i] = rows[i] - f * head
                inv[i] = inv[i] - f * head_inv
    u = jnp.concatenate(rows, axis=0)
    w = jnp.concatenate(inv, axis=0)
    return u, w


def mm(a, b, ca=1, cb=0):
    return lax.dot_general(
        a, b, (((ca,), (cb,)), ((), ())),
        precision=lax.Precision.HIGHEST, preferred_element_type=F32,
    )


def factor_half(a):
    u, w = eliminate(a)
    r = lax.broadcasted_iota(jnp.int32, (128, 128), 0)
    c = lax.broadcasted_iota(jnp.int32, (128, 128), 1)
    d = jnp.sum(jnp.where(r == c, u, 0.0), axis=1, keepdims=True)
    root = 1.0 / jnp.sqrt(d)
    return jnp.where(c >= r, u, 0.0) * root, w * root


def finish_kernel(gram, flat, basis, factor):
    unit = 1.0 / BEAMS**0.5
    r11, m11 = factor_half(gram[:128, :128])
    factor[:128, :128] = r11 * unit
    r12 = mm(m11, gram[:128, 128:])
    factor[:128, 128:] = r12 * unit
    factor[128:, :128] = jnp.zeros((128, 128), F32)
    r22, m22 = factor_half(gram[128:, 128:] - mm(r12, r12, 0, 0))
    factor[128:, 128:] = r22 * unit
    up = BEAMS**0.5
    left = mm(flat[:, :128], m11, 1, 1)
    basis[:, :128] = left * up
    basis[:, 128:] = mm(flat[:, 128:] - mm(left, r12), m22 * up, 1, 1)


def finish(gram, flat):
    vmem = pl.BlockSpec(memory_space=pltpu.VMEM)
    return pl.pallas_call(
        finish_kernel,
        out_shape=(
            jax.ShapeDtypeStruct((512, 256), F32),
            jax.ShapeDtypeStruct((256, 256), F32),
        ),
        in_specs=[vmem, vmem],
        out_specs=(vmem, vmem),
        compiler_params=pltpu.CompilerParams(vmem_limit_bytes=24 * MIB),
        name="finish",
    )(gram, flat)


def local(sketch, gains, coverage):
    halves = sketch.reshape(512, 2, W).transpose(1, 0, 2)
    shape = (4, 4, 2, 512, W)
    rounded, omega = first_pass(halves, gains, coverage)
    total = beam_pass(coverage, gains, rounded).reshape(shape)
    rounded, flat0 = second_pass(coverage, omega, gains, total)
    total = beam_pass(coverage, gains, rounded).reshape(shape)
    flat, gram = third_pass(total, flat0)
    basis, factor = finish(gram, flat)
    return basis.reshape(sketch.shape), factor


def solution(mesh):
    return jax.shard_map(
        local,
        mesh=mesh,
        in_specs=(P("beam", "pix", None), P("pix", "beam", None, None), P("pix", "beam")),
        out_specs=(P("beam", "pix", None), P()),
        check_vma=False,
    )
```
